32 devices in a mesh: tensor: 2 (over y), request: 16 (over z, x, core).
Axes of the slice: x: 2, y: 2, z: 4, core: 2. Of those that a mesh axis runs over, the one named last changes fastest.
Arguments:
- queries: bfloat16 [32, 16, 16384], P('request', None, 'tensor'), may hold values from -120 to 120
- cache_keys: bfloat16 [32, 256, 1024], P('request', None, 'tensor'), may hold values from -6 to 6
- cache_values: bfloat16 [32, 256, 1024], P('request', None, 'tensor'), may hold values from -6 to 6
- tree_keys: bfloat16 [32, 16, 1024], P('request', None, 'tensor'), may hold values from -6 to 6
- tree_values: bfloat16 [32, 16, 1024], P('request', None, 'tensor'), may hold values from -6 to 6
- cache_len: int32 [32], P('request'), may hold values from 64 to 256, as said below
- tree_parent: int32 [32, 16], P('request'), may hold values from 0 to 14, as said below
- residual: bfloat16 [32, 16, 16384], P('tensor', None, 'request'), may hold values from -6 to 6
- low_feats: bfloat16 [32, 16, 16384], P('tensor', None, 'request'), may hold values from -6 to 6
- mid_feats: bfloat16 [32, 16, 16384], P('tensor', None, 'request'), may hold values from -6 to 6
- out_proj: bfloat16 [16384, 16384], P('tensor', 'request'), may hold values from -1.25 to 1.25
- last_node: int32 [32], replicated, may hold values from 0 to 15
- draft_gain: float32 [16384], P('tensor'), may hold values from 0.1 to 1.9
- draft_join: bfloat16 [3, 16384, 16384], P(None, 'request', 'tensor'), may hold values from -0.24356964 to 0.24356964
Outputs:
- hidden: bfloat16 [32, 16, 16384], P('tensor', None, 'request')
- draft_features: bfloat16 [32, 16384], P('request', 'tensor')
The draws below stay inside these ranges and needn't reach their ends.
Inputs may be any that keep to these rules, and one draw needn't show every extreme that they name: `cache_len`: every request has between 64 and 256 filled cache positions, and some request has exactly 256. tree_parent[b, 0] = 0 and tree_parent[b, i] < i for i >= 1.
All inputs are finite; a program needn't handle non-finite values.
Results may differ from the reference program's by a relative error of at most 0.0075.
Values may be sent and summed in bfloat16 or wider, within the bound.
No kernel may reach another device: no remote copies, remote signals or barrier semaphores. Data moves between devices by JAX's collectives and lax.ppermute only.
A program may use at most 128 MiB of HBM per device.

```python
import jax
import jax.numpy as jnp
from jax import lax

D = 16384
HEADS = 128
KV_HEADS = 8
HEAD = 128
TREE = 16
CACHE = 256
REQS = 32


def key_table(key):
    table = jax.random.normal(jax.random.fold_in(key, 11), (REQS, CACHE, KV_HEADS * HEAD), jnp.float32)
    table = jnp.clip(table, -6.0, 6.0)
    return table


def draw_cache_keys(key, part):
    return key_table(key).astype(jnp.bfloat16)


def draw_queries(key, part):
    base = jax.random.normal(jax.random.fold_in(key, 13), (REQS, TREE, HEADS * HEAD), jnp.float32)
    base = jnp.clip(base, -6.0, 6.0)
    return base.astype(jnp.bfloat16)


def draw_cache_len(key, part):
    lengths = jax.random.randint(jax.random.fold_in(key, 21), (REQS,), CACHE // 4, CACHE + 1)
    fullest = jax.random.randint(jax.random.fold_in(key, 22), (), 0, REQS)
    return jnp.where(jnp.arange(REQS) == fullest, CACHE, lengths).astype(jnp.int32)


def draw_tree_parent(key, part):
    nodes = jnp.arange(TREE, dtype=jnp.int32)
    raw = jax.random.randint(jax.random.fold_in(key, 31), (REQS, TREE), 0, 1048576)
    parents = (raw % jnp.maximum(nodes, 1)[None, :]).astype(jnp.int32)
    chain = jax.random.randint(jax.random.fold_in(key, 32), (), 0, REQS)
    chain_row = jnp.maximum(nodes - 1, 0)
    return jnp.where((jnp.arange(REQS) == chain)[:, None], chain_row[None, :], parents).astype(jnp.int32)


def draw_draft_join(key, part):
    place = jnp.arange(D, dtype=jnp.float32) / D
    base = jnp.clip(jax.random.normal(jax.random.fold_in(key, 42), (3, D, D), jnp.float32), -6.0, 6.0)
    rise = jnp.exp(place * 1.0986123)
    scale = rise * (3.0 * D) ** (-0.5)
    return (base * scale[None, None, :]).astype(jnp.bfloat16)


def set_ends(values, own_key, low, high):
    extent = values.shape
    spot = [jax.random.randint(jax.random.fold_in(own_key, axis), (), 0, extent[axis]) for axis in range(len(extent))]
    values = values.at[tuple(spot)].set(low)
    longest = extent.index(max(extent))
    spot[longest] = (spot[longest] + 1) % extent[longest]
    return values.at[tuple(spot)].set(high)


def shard_levels(stream_key, extent, cuts, least, top_value):
    level = 1.0
    for dim, blocks in cuts:
        draws = jax.random.uniform(jax.random.fold_in(jax.random.fold_in(stream_key, 6), dim), (blocks,), jnp.float32, least / len(cuts), top_value / len(cuts))
        level = level * jnp.repeat(jnp.exp(draws), extent[dim] // blocks).reshape((-1,) + (1,) * (len(extent) - 1 - dim))
    return level


def gaussian(stream_key, dims, width, most, cuts=(), kind=jnp.bfloat16):
    values = jax.random.normal(stream_key, dims, jnp.float32) * width
    if len(cuts) > 0:
        values = shard_levels(stream_key, dims, cuts, -0.22, 0.18) * values
    return jnp.clip(values, min=-most, max=most).astype(kind)


def setup_inputs(seed: int = 0) -> dict:
    keys = jax.random.split(jax.random.key(seed), 15)
    return {
        "queries": draw_queries(jax.random.fold_in(keys[14], 71), 0),
        "cache_keys": draw_cache_keys(jax.random.fold_in(keys[14], 71), 0),
        "cache_values": gaussian(keys[2], (REQS, CACHE, KV_HEADS * HEAD), 1.0, 6.0, ((0, 16), (2, 2))),
        "tree_keys": gaussian(keys[3], (REQS, TREE, KV_HEADS * HEAD), 1.0, 6.0, ((0, 16), (2, 2))),
        "tree_values": gaussian(keys[4], (REQS, TREE, KV_HEADS * HEAD), 1.0, 6.0, ((0, 16), (2, 2))),
        "cache_len": draw_cache_len(jax.random.fold_in(keys[14], 71), 0),
        "tree_parent": draw_tree_parent(jax.random.fold_in(keys[14], 71), 0),
        "residual": gaussian(keys[7], (REQS, TREE, D), 0.5, 6.0, ((0, 2), (2, 16))),
        "low_feats": gaussian(keys[8], (REQS, TREE, D), 1.0, 6.0, ((0, 2), (2, 16))),
        "mid_feats": gaussian(keys[9], (REQS, TREE, D), 1.0, 6.0, ((0, 2), (2, 16))),
        "out_proj": gaussian(keys[10], (HEADS * HEAD, D), 0.08, 1.25, ((0, 2), (1, 16))),
        "last_node": set_ends(jax.random.randint(keys[11], (REQS,), 0, TREE), jax.random.fold_in(keys[11], 1), 0, TREE - 1).astype(jnp.int32),
        "draft_gain": jnp.clip(1.0 + 0.18 * jax.random.normal(keys[12], (D,), jnp.float32), 0.1, 1.9),
        "draft_join": draw_draft_join(jax.random.fold_in(keys[14], 71), 0),
    }


def ancestors(parents):
    nodes = jnp.arange(TREE, dtype=jnp.int32)
    step_matrix = (parents[:, None] == nodes[None, :]).astype(jnp.float32)
    reach = jnp.eye(TREE, dtype=jnp.float32)
    walker = reach
    for hop in range(TREE - 1):
        walker = jnp.dot(walker, step_matrix, precision=lax.Precision.HIGHEST)
        reach = jnp.maximum(reach, walker)
    return (reach > 0.5).astype(jnp.int32)

def verify_request(inputs):
    query_rows, keys_cache, values_cache, keys_tree, values_tree, length, parents = inputs
    kv_count = keys_cache.shape[-1] // HEAD
    group = HEADS // KV_HEADS
    factor = HEAD ** (-0.5)
    query_heads = query_rows.reshape(TREE, kv_count, group, HEAD).astype(jnp.float32)
    cache_k = keys_cache.reshape(CACHE, kv_count, HEAD).astype(jnp.float32)
    cache_v = values_cache.reshape(CACHE, kv_count, HEAD).astype(jnp.float32)
    tree_k = keys_tree.reshape(TREE, kv_count, HEAD).astype(jnp.float32)
    tree_v = values_tree.reshape(TREE, kv_count, HEAD).astype(jnp.float32)
    high = lax.Precision.HIGHEST
    score_cache = jnp.einsum('tgqd,pgd->gqtp', query_heads, cache_k, precision=high) * factor
    live = jnp.arange(CACHE, dtype=jnp.int32) < length
    score_cache = jnp.where(live, score_cache, -1e+30)
    score_tree = jnp.einsum('tgqd,jgd->gqtj', query_heads, tree_k, precision=high) * factor
    score_tree = jnp.where(ancestors(parents) == 1, score_tree, -1e+30)
    top = jnp.maximum(lax.optimization_barrier(jnp.max(score_cache, axis=-1)), lax.optimization_barrier(jnp.max(score_tree, axis=-1)))
    exp_cache = jnp.exp(score_cache - top[..., None])
    exp_tree = jnp.exp(score_tree - top[..., None])
    total = lax.optimization_barrier(jnp.sum(exp_cache, axis=-1)) + lax.optimization_barrier(jnp.sum(exp_tree, axis=-1))
    weight_cache = (exp_cache / total[..., None]).astype(jnp.bfloat16).astype(jnp.float32)
    weight_tree = (exp_tree / total[..., None]).astype(jnp.bfloat16).astype(jnp.float32)
    mixed = jnp.einsum('gqtp,pgd->tgqd', weight_cache, cache_v, precision=high)
    mixed = mixed + jnp.einsum('gqtj,jgd->tgqd', weight_tree, tree_v, precision=high)
    return mixed.reshape(TREE, kv_count * group * HEAD).astype(jnp.bfloat16)

def reference(queries, cache_keys, cache_values, tree_keys, tree_values, cache_len, tree_parent, residual, low_feats, mid_feats, out_proj, last_node, draft_gain, draft_join):
    heads_out = lax.map(verify_request, (queries, cache_keys, cache_values, tree_keys, tree_values, cache_len, tree_parent))
    flat_rows = heads_out.reshape(REQS * TREE, HEADS * HEAD)
    projected = jnp.dot(flat_rows, out_proj, preferred_element_type=jnp.float32)
    hidden = (residual.reshape(REQS * TREE, D).astype(jnp.float32) + projected).astype(jnp.bfloat16)
    hidden = hidden.reshape(REQS, TREE, D)
    chosen = last_node[:, None] == jnp.arange(TREE, dtype=jnp.int32)[None, :]

    def pick(rows):
        return lax.optimization_barrier(jnp.sum(jnp.where(chosen[:, :, None], rows.astype(jnp.float32), 0.0), axis=1)).astype(jnp.bfloat16)
    joined = jnp.dot(pick(low_feats), draft_join[0], preferred_element_type=jnp.float32)
    joined = joined + jnp.dot(pick(mid_feats), draft_join[1], preferred_element_type=jnp.float32)
    joined = joined + jnp.dot(pick(hidden), draft_join[2], preferred_element_type=jnp.float32)
    row_scale = lax.rsqrt(lax.optimization_barrier(jnp.sum(joined * joined, axis=1)) / D + 1e-05)
    features = (joined * row_scale[:, None] * draft_gain[None, :]).astype(jnp.bfloat16)
    return (hidden, features)
```

```python
import functools

import jax
import jax.numpy as jnp
from jax import lax
from jax.experimental import pallas as pl
from jax.experimental.pallas import tpu as pltpu
from jax.sharding import PartitionSpec as P

D = 16384
HEADS = 128
KV_HEADS = 8
HEAD = 128
TREE = 16
GROUP = HEADS // KV_HEADS
FACTOR = HEAD ** (-0.5)
LIMIT = 44 * 1024 * 1024
BF = jnp.bfloat16
F32 = jnp.float32


def params(grid_dims=1):
    return pltpu.CompilerParams(
        vmem_limit_bytes=LIMIT, dimension_semantics=("arbitrary",) * grid_dims
    )


def attention_kernel(len_ref, last_ref, parent_ref, q_ref, ck_ref, cv_ref, tk_ref, tv_ref, o_ref, pick_ref, vis_ref):
    g, b = pl.program_id(0), pl.program_id(1)

    @pl.when(g == 0)
    def _():
        cols = lax.broadcasted_iota(jnp.int32, (TREE, TREE), 1)
        rows = lax.broadcasted_iota(jnp.int32, (TREE, TREE), 0)
        reach = jnp.where((parent_ref[0] == cols) | (rows == cols), 1.0, 0.0).astype(F32)
        for _ in range(4):
            half = reach.astype(BF)
            reach = jnp.minimum(jnp.dot(half, half, preferred_element_type=F32), 1.0)
        vis_ref[b] = reach

    q = q_ref[0]
    stacked = jnp.concatenate([q[:, h * HEAD : (h + 1) * HEAD] for h in range(GROUP)], axis=0)
    dims = (((1,), (1,)), ((), ()))
    s_cache = lax.dot_general(stacked, ck_ref[0], dims, preferred_element_type=F32) * FACTOR
    s_tree = lax.dot_general(stacked, tk_ref[0], dims, preferred_element_type=F32) * FACTOR
    live = lax.broadcasted_iota(jnp.int32, (1, s_cache.shape[1]), 1) < len_ref[b]
    s_cache = jnp.where(live, s_cache, -1e30)
    seen = jnp.concatenate([vis_ref[b]] * GROUP, axis=0) > 0.5
    s_tree = jnp.where(seen, s_tree, -1e30)
    top = jnp.maximum(
        jnp.max(s_cache, axis=1, keepdims=True), jnp.max(s_tree, axis=1, keepdims=True)
    )
    e_cache = jnp.exp(s_cache - top)
    e_tree = jnp.exp(s_tree - top)
    total = jnp.sum(e_cache, axis=1, keepdims=True) + jnp.sum(e_tree, axis=1, keepdims=True)
    inverse = 1.0 / total
    w_cache = (e_cache * inverse).astype(BF)
    w_tree = (e_tree * inverse).astype(BF)
    mixed = jnp.dot(w_cache, cv_ref[0], preferred_element_type=F32)
    mixed = mixed + jnp.dot(w_tree, tv_ref[0], preferred_element_type=F32)
    chosen = lax.broadcasted_iota(jnp.int32, (TREE, 1), 0) == last_ref[b]
    picks = []
    for h in range(GROUP):
        block = mixed[h * TREE : (h + 1) * TREE]
        o_ref[0, :, h * HEAD : (h + 1) * HEAD] = block.astype(BF)
        picks.append(jnp.sum(jnp.where(chosen, block, 0.0), axis=0, keepdims=True))
    row = jnp.concatenate(picks, axis=1)
    which = lax.broadcasted_iota(jnp.int32, pick_ref.shape, 0) == b
    pick_ref[...] = jnp.where(which, row, pick_ref[...].astype(F32)).astype(BF)


def attention(queries, ck, cv, tk, tv, lengths, parents, last):
    count, _, width = queries.shape
    cache = ck.shape[1]
    groups = ck.shape[2] // HEAD
    lanes = GROUP * HEAD
    smem = pl.BlockSpec(memory_space=pltpu.SMEM)
    wide = pl.BlockSpec((1, TREE, lanes), lambda g, b: (b, 0, g))
    long = pl.BlockSpec((1, cache, HEAD), lambda g, b: (b, 0, g))
    short = pl.BlockSpec((1, TREE, HEAD), lambda g, b: (b, 0, g))
    return pl.pallas_call(
        attention_kernel,
        grid=(groups, count),
        in_specs=[smem, smem, pl.BlockSpec((1, TREE, 1), lambda g, b: (b, 0, 0)), wide, long, long, short, short],
        out_specs=[wide, pl.BlockSpec((count, lanes), lambda g, b: (0, g))],
        out_shape=[
            jax.ShapeDtypeStruct(queries.shape, BF),
            jax.ShapeDtypeStruct((count, width), BF),
        ],
        scratch_shapes=[pltpu.VMEM((count, TREE, TREE), F32)],
        compiler_params=params(2),
        name="attention",
    )(lengths, last, parents[:, :, None], queries, ck, cv, tk, tv)


def pick_kernel(row_ref, low_ref, mid_ref, res_ref, feats_ref, res_out_ref):
    rows = low_ref.shape[0]
    count = row_ref.shape[0]
    hot = row_ref[...] == lax.broadcasted_iota(jnp.int32, (count, rows), 1)
    hot = jnp.where(hot, 1.0, 0.0).astype(BF)
    feats_ref[:count] = jnp.dot(hot, low_ref[...], preferred_element_type=F32).astype(BF)
    feats_ref[count:] = jnp.dot(hot, mid_ref[...], preferred_element_type=F32).astype(BF)
    res_out_ref[...] = jnp.dot(hot, res_ref[...], preferred_element_type=F32)


def pick(row_ids, low, mid, res):
    count, columns = row_ids.shape[0], low.shape[1]
    return pl.pallas_call(
        pick_kernel,
        out_shape=[
            jax.ShapeDtypeStruct((2 * count, columns), BF),
            jax.ShapeDtypeStruct((count, columns), F32),
        ],
        compiler_params=params(0),
        name="pick",
    )(row_ids, low, mid, res)


def project(name, blocks, weights, extras, finish, outs, step=1024):
    rows = sum(x.shape[0] for x in blocks)
    depth, columns = weights.shape
    steps = depth // step
    n = len(blocks)
    m = len(extras)

    def kernel(*refs):
        xs, w, more = refs[:n], refs[n], refs[n + 1 : n + 1 + m]
        results, total = refs[n + 1 + m : -1], refs[-1]
        k = pl.program_id(0)
        x = jnp.concatenate([r[...] for r in xs], axis=0)
        part = jnp.dot(x, w[...], preferred_element_type=F32)

        @pl.when(k == 0)
        def _():
            total[...] = part

        @pl.when(k > 0)
        def _():
            total[...] += part

        @pl.when(k == steps - 1)
        def _():
            finish(total, more, results)

    extra_specs, extra_args = [], []
    for extra in extras:
        array, spec = extra
        extra_args.append(array)
        extra_specs.append(spec)
    return pl.pallas_call(
        kernel,
        grid=(steps,),
        in_specs=[pl.BlockSpec((x.shape[0], step), lambda k: (0, k)) for x in blocks]
        + [pl.BlockSpec((step, columns), lambda k: (k, 0))]
        + extra_specs,
        out_specs=[pl.BlockSpec(o.shape, lambda k: (0, 0)) for o in outs],
        out_shape=outs,
        scratch_shapes=[pltpu.VMEM((rows, columns), F32)],
        compiler_params=params(1),
        cost_estimate=pl.CostEstimate(
            flops=2 * rows * depth * columns,
            bytes_accessed=2 * depth * columns + 2 * rows * depth,
            transcendentals=0,
        ),
        name=name,
    )(*blocks, weights, *extra_args)


def whole(array):
    return (array, pl.BlockSpec(array.shape, lambda k: (0,) * array.ndim))


def scalars(array):
    return (array, pl.BlockSpec(memory_space=pltpu.SMEM))


def join_features(own, other, join, step=512):
    count = own.shape[0] // 2
    depth, columns = join.shape[1:]

    def kernel(a_ref, b_ref, w_ref, o_ref):
        x = a_ref[...] + b_ref[...]
        o_ref[...] = jnp.dot(x[:count], w_ref[0], preferred_element_type=F32) + jnp.dot(
            x[count:], w_ref[1], preferred_element_type=F32
        )

    return pl.pallas_call(
        kernel,
        grid=(columns // step,),
        in_specs=[
            pl.BlockSpec(own.shape, lambda n: (0, 0)),
            pl.BlockSpec(own.shape, lambda n: (0, 0)),
            pl.BlockSpec((2, depth, step), lambda n: (0, 0, n)),
        ],
        out_specs=pl.BlockSpec((count, step), lambda n: (0, n)),
        out_shape=jax.ShapeDtypeStruct((count, columns), F32),
        compiler_params=params(1),
        cost_estimate=pl.CostEstimate(
            flops=4 * count * depth * columns,
            bytes_accessed=4 * depth * columns,
            transcendentals=0,
        ),
        name="join_features",
    )(own, other, join)


def join_hidden(own, other, before, join, step=1024):
    count = own.shape[0]
    depth, columns = join.shape[1:]
    half = count // 2

    def kernel(a_ref, b_ref, before_ref, w_ref, keep_ref, send_ref):
        x = (a_ref[...] + b_ref[...]).astype(BF)
        y = jnp.dot(x, w_ref[0], preferred_element_type=F32) + before_ref[...]
        keep_ref[...] = y[:half]
        send_ref[...] = y[half:].astype(BF)

    return pl.pallas_call(
        kernel,
        grid=(columns // step,),
        in_specs=[
            pl.BlockSpec(own.shape, lambda n: (0, 0)),
            pl.BlockSpec(own.shape, lambda n: (0, 0)),
            pl.BlockSpec((count, step), lambda n: (0, n)),
            pl.BlockSpec((1, depth, step), lambda n: (2, 0, n)),
        ],
        out_specs=[
            pl.BlockSpec((half, step), lambda n: (0, n)),
            pl.BlockSpec((half, step), lambda n: (0, n)),
        ],
        out_shape=[
            jax.ShapeDtypeStruct((half, columns), F32),
            jax.ShapeDtypeStruct((half, columns), BF),
        ],
        compiler_params=params(1),
        cost_estimate=pl.CostEstimate(
            flops=2 * count * depth * columns,
            bytes_accessed=2 * depth * columns + 6 * count * columns,
            transcendentals=0,
        ),
        name="join_hidden",
    )(own, other, before, join)


def finish_hidden(places, keep_b, got_b, keep_c, got_c, residual, rows):
    columns = residual.shape[1]
    n_b, n_c = keep_b.shape[0] // rows, keep_c.shape[0] // rows

    def kernel(place_ref, kb, gb, kc, gc, res, out):
        i = pl.program_id(0)

        @pl.when(i < n_b)
        def _():
            out[...] = (res[...].astype(F32) + (kb[...] + gb[...].astype(F32))).astype(BF)

        @pl.when(i >= n_b)
        def _():
            out[...] = (res[...].astype(F32) + (kc[...] + gc[...].astype(F32))).astype(BF)

    block = (rows, columns)
    early = lambda i, p: (jnp.minimum(i, n_b - 1), 0)
    late = lambda i, p: (jnp.maximum(i - n_b, 0), 0)
    moved = lambda i, p: (p[i], 0)
    return pl.pallas_call(
        kernel,
        grid_spec=pltpu.PrefetchScalarGridSpec(
            num_scalar_prefetch=1,
            grid=(n_b + n_c,),
            in_specs=[
                pl.BlockSpec(block, early),
                pl.BlockSpec(block, early),
                pl.BlockSpec(block, late),
                pl.BlockSpec(block, late),
                pl.BlockSpec(block, moved),
            ],
            out_specs=pl.BlockSpec(block, moved),
        ),
        out_shape=jax.ShapeDtypeStruct(residual.shape, BF),
        compiler_params=params(1),
        name="finish_hidden",
    )(places, keep_b, got_b, keep_c, got_c, residual)


CHIPS = 8


def chip_of(position):
    return (position, 0) if position < 4 else (7 - position, 1)


def device_of(position, core):
    z, x = chip_of(position % CHIPS)
    return (z * 2 + x) * 2 + core


def ring_body(
    queries,
    cache_keys,
    cache_values,
    tree_keys,
    tree_values,
    cache_len,
    tree_parent,
    residual,
    low_feats,
    mid_feats,
    out_proj,
    last_node,
    draft_gain,
    draft_join,
):
    request = lax.axis_index("request")
    side = lax.axis_index("tensor")
    size = lax.axis_size("request")
    own_count = queries.shape[0]
    columns = residual.shape[2]
    all_req = last_node.shape[0]
    side_rows = residual.shape[0] * TREE
    block_rows = own_count * TREE

    forward = [(device_of(p, c), device_of(p + 1, c)) for p in range(CHIPS) for c in range(2)]
    backward = [(b, a) for a, b in forward]
    ahead = lambda v: lax.ppermute(v, "request", forward)
    back = lambda v: lax.ppermute(v, "request", backward)
    swap_core = lambda v: lax.ppermute(v, "request", [(r, r ^ 1) for r in range(size)])
    swap_x = lambda v: lax.ppermute(v, "request", [(r, r ^ 2) for r in range(size)])
    shift_z = lambda v, k: lax.ppermute(v, "request", [(r, (r + 4 * k) % size) for r in range(size)])
    swap_side = lambda v: lax.ppermute(v, "tensor", [(0, 1), (1, 0)])

    core, x, z = request % 2, (request // 2) % 2, request // 4
    position = jnp.where(x == 0, z, 7 - z)
    pairs = jnp.array([-1, 1, -2, 0], jnp.int32)
    first = (position + pairs + CHIPS) % CHIPS
    first_side = ((first + 2) // 4) % 2
    flags = (first_side == side).astype(jnp.int32)
    kept = jnp.where(flags == 1, first, (first + 4) % CHIPS)
    kept_chip = jnp.where(kept < 4, kept * 2, (7 - kept) * 2 + 1)
    kept_device = kept_chip[:, None] * 2 + jnp.stack([core, 1 - core])[None, :]
    places = (kept_device - side * (size // 2)).reshape(-1).astype(jnp.int32)

    order = jnp.arange(all_req, dtype=jnp.int32)
    rel_core, rel_x, rel_z, within = order // 16, (order // 8) % 2, (order // 2) % 4, order % 2
    of_z, of_x, of_core = (z - rel_z + 4) % 4, (x + rel_x) % 2, (core + rel_core) % 2
    req = ((of_z * 2 + of_x) * 2 + of_core) * own_count + within
    last_rel = jnp.sum(jnp.where(req[:, None] == order[None, :], last_node[None, :], 0), axis=1)
    row_ids = (req * TREE + last_rel - side * side_rows)[:, None]
    own_last = lax.dynamic_slice_in_dim(last_node, request * own_count, own_count, 0)

    feats, res_rows = pick(
        row_ids,
        low_feats.reshape(-1, columns),
        mid_feats.reshape(-1, columns),
        residual.reshape(-1, columns),
    )
    feats_other = swap_side(feats)

    heads, picked = attention(
        queries, cache_keys, cache_values, tree_keys, tree_values, cache_len, tree_parent, own_last
    )
    h = heads.reshape(block_rows, -1)

    by_z = jnp.concatenate([picked] + [shift_z(picked, k) for k in range(1, 4)], axis=0)
    by_x = jnp.concatenate([by_z, swap_x(by_z)], axis=0)

    f1, b1 = ahead(h), back(h)
    hs = swap_core(h)
    picked_other = swap_core(by_x)

    joined_feats = join_features(feats, feats_other, draft_join)

    f2, b2 = ahead(f1), back(b1)
    f1s, b1s = swap_core(f1), swap_core(b1)

    def finish_a(total, more, results):
        results[0][...] = total[: 6 * block_rows]
        results[1][...] = total[6 * block_rows :] + more[0][...]

    part_a, part_picked = project(
        "project_a",
        [h, hs, f1, f1s, b1, b1s, by_x, picked_other],
        out_proj,
        [whole(res_rows)],
        finish_a,
        [
            jax.ShapeDtypeStruct((6 * block_rows, columns), F32),
            jax.ShapeDtypeStruct((all_req, columns), F32),
        ],
    )
    part_other = swap_side(part_picked)

    f3, b3 = ahead(f2), back(b2)
    f2s, b2s = swap_core(f2), swap_core(b2)

    keep16, send16 = join_hidden(part_picked, part_other, joined_feats, draft_join)
    got16 = swap_core(send16)

    f4, b4 = ahead(f3[:TREE]), back(b3[TREE:])
    f3s, b3s = swap_core(f3), swap_core(b3)

    two = 2 * block_rows

    def finish_b(total, more, results):
        flag, before = more
        keep, send = results
        early = [before[two : 2 * two], before[2 * two : 3 * two]]
        late = [total[i * two : (i + 1) * two] for i in range(4)]
        for i, (u, v) in enumerate([(early[0], late[3]), (early[1], late[2]), (late[0], late[1])]):
            mine = flag[i] == 1
            keep[i * two : (i + 1) * two] = jnp.where(mine, u, v)
            send[i * two : (i + 1) * two] = jnp.where(mine, v, u).astype(BF)

    keep_b, send_b = project(
        "project_b",
        [f2, f2s, b2, b2s, f3, f3s, b3, b3s],
        out_proj,
        [scalars(flags), whole(part_a)],
        finish_b,
        [
            jax.ShapeDtypeStruct((3 * two, columns), F32),
            jax.ShapeDtypeStruct((3 * two, columns), BF),
        ],
    )
    got_b = swap_side(send_b)

    f4s, b4s = swap_core(f4), swap_core(b4)

    def finish_c(total, more, results):
        flag, before = more
        keep, send = results
        mine = flag[3] == 1
        u, v = before[...], total[...]
        keep[...] = jnp.where(mine, u, v)
        send[...] = jnp.where(mine, v, u).astype(BF)

    keep_c, send_c = project(
        "project_c",
        [f4, b4, f4s, b4s],
        out_proj,
        [scalars(flags), (part_a, pl.BlockSpec((two, columns), lambda k: (0, 0)))],
        finish_c,
        [
            jax.ShapeDtypeStruct((two, columns), F32),
            jax.ShapeDtypeStruct((two, columns), BF),
        ],
    )
    got_c = swap_side(send_c)

    hidden = finish_hidden(
        places, keep_b, got_b, keep_c, got_c, residual.reshape(-1, columns), block_rows
    ).reshape(residual.shape)

    sum16 = keep16 + got16.astype(F32)
    sum8 = sum16[:8] + swap_x(sum16[8:].astype(BF)).astype(F32)
    joined = sum8[:own_count]
    for k in range(1, 4):
        send = sum8[k * own_count : (k + 1) * own_count].astype(BF)
        joined = joined + shift_z(send, 4 - k).astype(F32)
    squares = jnp.sum(joined * joined, axis=1, keepdims=True)
    squares = squares + swap_side(squares)
    row_scale = lax.rsqrt(squares / D + 1e-05)
    features = (joined * row_scale * draft_gain[None, :]).astype(BF)
    return (hidden, features)


def any_body(
    queries,
    cache_keys,
    cache_values,
    tree_keys,
    tree_values,
    cache_len,
    tree_parent,
    residual,
    low_feats,
    mid_feats,
    out_proj,
    last_node,
    draft_gain,
    draft_join,
):
    own_count = queries.shape[0]
    first_own = lax.axis_index("request") * own_count
    own_last = lax.dynamic_slice_in_dim(last_node, first_own, own_count, 0)
    heads, _ = attention(
        queries, cache_keys, cache_values, tree_keys, tree_values, cache_len, tree_parent, own_last
    )
    flat_rows = heads.reshape(-1, heads.shape[-1])
    partial_value = jnp.dot(
        lax.all_gather(flat_rows, "request", axis=0, tiled=True),
        out_proj,
        preferred_element_type=F32,
    )
    summed = lax.psum_scatter(partial_value, "tensor", scatter_dimension=0, tiled=True)
    local_req = residual.shape[0]
    columns = residual.shape[2]
    hidden = (residual.reshape(-1, columns).astype(F32) + summed).astype(BF)
    hidden = hidden.reshape(residual.shape)
    first_req = lax.axis_index("tensor") * local_req
    chosen_all = last_node[:, None] == jnp.arange(TREE, dtype=jnp.int32)[None, :]
    own_chosen = lax.dynamic_slice_in_dim(chosen_all, first_req, local_req, 0)

    def choose(rows):
        return jnp.sum(jnp.where(own_chosen[:, :, None], rows.astype(F32), 0.0), axis=1).astype(BF)

    rows = jnp.stack((choose(low_feats), choose(mid_feats), choose(hidden)), axis=1)
    stacked = lax.all_gather(rows, "tensor", axis=0, tiled=True)
    joined_part = jnp.einsum("bsk,skn->bn", stacked, draft_join, preferred_element_type=F32)
    joined = lax.psum_scatter(joined_part, "request", scatter_dimension=0, tiled=True)
    squares = lax.psum(jnp.sum(joined * joined, axis=1), "tensor")
    row_scale = lax.rsqrt(squares / D + 1e-05)
    features = (joined * row_scale[:, None] * draft_gain[None, :]).astype(BF)
    return (hidden, features)


def solution(mesh):
    small = mesh.shape["tensor"] == 2 and mesh.shape["request"] == 2 * CHIPS
    return jax.shard_map(
        ring_body if small else any_body,
        mesh=mesh,
        in_specs=(
            P("request", None, "tensor"),
            P("request", None, "tensor"),
            P("request", None, "tensor"),
            P("request", None, "tensor"),
            P("request", None, "tensor"),
            P("request"),
            P("request", None),
            P("tensor", None, "request"),
            P("tensor", None, "request"),
            P("tensor", None, "request"),
            P("tensor", "request"),
            P(),
            P("tensor"),
            P(None, "request", "tensor"),
        ),
        out_specs=(P("tensor", None, "request"), P("request", "tensor")),
        check_vma=False,
    )
```

```python
import jax
import jax.numpy as jnp
from jax import lax
from jax.experimental import pallas as pl
from jax.experimental.pallas import tpu as pltpu
from jax.sharding import PartitionSpec as P

D = 16384
HEADS = 128
KV_HEADS = 8
HEAD = 128
TREE = 16
GROUP = HEADS // KV_HEADS
FACTOR = HEAD ** (-0.5)
MIB = 1024 * 1024
ATTENTION_MIB = 58
EARLY = pl.CostEstimate(flops=1, bytes_accessed=1, transcendentals=0)
BF = jnp.bfloat16
F32 = jnp.float32


def small_params(limit=12):
    return pltpu.CompilerParams(vmem_limit_bytes=int(limit * MIB))


def stream_params():
    return pltpu.CompilerParams(
        vmem_limit_bytes=16 * MIB, dimension_semantics=("arbitrary",)
    )


CHIPS = 8


def chip_of(position):
    return (position, 0) if position < 4 else (7 - position, 1)


def device_of(position, core):
    z, x = chip_of(position % CHIPS)
    return (z * 2 + x) * 2 + core


def coordinates(request):
    core, x, z = request & 1, (request >> 1) & 1, request >> 2
    return core, x, z, jnp.where(x == 0, z, 7 - z)


PAIRS = ((-1, 3), (1, -3), (-2, 2), (0, 4))


def first_is_mine(pair, position, side):
    first = (position + PAIRS[pair][0] + CHIPS) & 7
    return first, (((first + 2) >> 2) & 1) == side


HBM = pl.BlockSpec(memory_space=pltpu.HBM)
VMEM = pl.BlockSpec(memory_space=pltpu.VMEM)
SMEM = pl.BlockSpec(memory_space=pltpu.SMEM)


def attention(queries, ck, cv, tk, tv, lengths, parents, last, picks=None):
    count, _, width = queries.shape
    cache = ck.shape[1]
    groups = ck.shape[2] // HEAD
    lanes = GROUP * HEAD
    sources = (parents, queries, ck, tk, cv, tv) + (picks or ())
    all_req = last.shape[0]

    def kernel(len_ref, last_ref, *refs):
        n = len(sources)
        here, refs = refs[:n], refs[n:]
        if picks:
            row_ref, o_ref, pick_ref, feats_ref, res_out_ref = refs[:5]
            refs = refs[5:]
        else:
            o_ref, pick_ref = refs[:2]
            refs = refs[2:]
        held, sem = refs[:n], refs[n]
        copies = [pltpu.make_async_copy(a, v, sem.at[i]) for i, (a, v) in enumerate(zip(here, held))]
        for c in copies:
            c.start()
        parent, q_ref, ck_ref, tk_ref, cv_ref, tv_ref = held[:6]
        first = lax.axis_index("request") * count
        copies[0].wait()
        up = lax.broadcasted_iota(jnp.int32, (TREE, TREE), 0)
        node = lax.broadcasted_iota(jnp.int32, (TREE, TREE), 1)
        spread = lax.broadcasted_iota(jnp.int32, (GROUP * TREE, TREE), 0) % TREE
        spread = spread == lax.broadcasted_iota(jnp.int32, (GROUP * TREE, TREE), 1)
        spread = jnp.where(spread, 1.0, 0.0).astype(BF)
        dims = (((1,), (1,)), ((), ()))
        seen = []
        for b in range(count):
            reach = jnp.where((parent[b : b + 1] == up) | (up == node), 1.0, 0.0).astype(BF)
            for _ in range(4):
                paths = jnp.dot(reach, reach, preferred_element_type=F32)
                reach = jnp.minimum(paths, 1.0).astype(BF)
            seen.append(lax.dot_general(spread, reach, dims, preferred_element_type=F32) > 0.5)
        for c in copies[1:6]:
            c.wait()
        for b in range(count):
            live = lax.broadcasted_iota(jnp.int32, (1, cache), 1) < len_ref[b]
            chosen = lax.broadcasted_iota(jnp.int32, (TREE, 1), 0) == last_ref[first + b]
            for g in range(groups):
                head = slice(g * HEAD, (g + 1) * HEAD)
                base = g * lanes
                q = jnp.concatenate(
                    [q_ref[b, :, base + h * HEAD : base + (h + 1) * HEAD] for h in range(GROUP)],
                    axis=0,
                )
                s_cache = lax.dot_general(q, ck_ref[b, :, head], dims, preferred_element_type=F32)
                s_tree = lax.dot_general(q, tk_ref[b, :, head], dims, preferred_element_type=F32)
                s_cache = jnp.where(live, s_cache * FACTOR, -1e30)
                s_tree = jnp.where(seen[b], s_tree * FACTOR, -1e30)
                top = jnp.maximum(
                    jnp.max(s_cache, axis=1, keepdims=True), jnp.max(s_tree, axis=1, keepdims=True)
                )
                e_cache = jnp.exp(s_cache - top)
                e_tree = jnp.exp(s_tree - top)
                total = jnp.sum(e_cache, axis=1, keepdims=True) + jnp.sum(
                    e_tree, axis=1, keepdims=True
                )
                inverse = 1.0 / total
                w_cache = (e_cache * inverse).astype(BF)
                w_tree = (e_tree * inverse).astype(BF)
                mixed = jnp.dot(w_cache, cv_ref[b, :, head], preferred_element_type=F32)
                mixed = mixed + jnp.dot(w_tree, tv_ref[b, :, head], preferred_element_type=F32)
                for h in range(GROUP):
                    block = mixed[h * TREE : (h + 1) * TREE]
                    where = slice(base + h * HEAD, base + (h + 1) * HEAD)
                    o_ref[b * TREE : (b + 1) * TREE, where] = block.astype(BF)
                    pick_ref[b : b + 1, where] = jnp.sum(
                        jnp.where(chosen, block, 0.0), axis=0, keepdims=True
                    ).astype(BF)

        if picks:
            side_rows = picks[0].shape[0]
            core, x, z, _ = coordinates(lax.axis_index("request"))
            order = lax.broadcasted_iota(jnp.int32, (all_req, all_req), 0)
            of_core, of_x = core ^ (order >> 4), x ^ ((order >> 3) & 1)
            of_z = z ^ ((order >> 1) & 3)
            req = ((of_z * 2 + of_x) * 2 + of_core) * count + (order & 1)
            named = req == lax.broadcasted_iota(jnp.int32, (all_req, all_req), 1)
            last_rel = jnp.sum(jnp.where(named, row_ref[...], 0), axis=1, keepdims=True)
            rows = req[:, :1] * TREE + last_rel - lax.axis_index("tensor") * side_rows
            hot = rows == lax.broadcasted_iota(jnp.int32, (all_req, side_rows), 1)
            hot = jnp.where(hot, 1.0, 0.0).astype(BF)
            for c in copies[6:9]:
                c.wait()
            for i in range(2):
                feats_ref[i * all_req : (i + 1) * all_req] = jnp.dot(
                    hot, held[6 + i][...], preferred_element_type=F32
                ).astype(BF)
            res_out_ref[...] = jnp.dot(hot, held[8][...], preferred_element_type=F32)

    arrays = [lengths, last, *sources]
    in_specs = [SMEM, SMEM] + [HBM] * len(sources)
    outs = [
        jax.ShapeDtypeStruct((count * TREE, width), BF),
        jax.ShapeDtypeStruct((count, width), BF),
    ]
    scratch = [pltpu.VMEM(a.shape, a.dtype) for a in sources]
    scratch.append(pltpu.SemaphoreType.DMA((len(sources),)))
    if picks:
        arrays.append(last[None, :])
        in_specs.append(VMEM)
        columns = picks[0].shape[1]
        outs += [
            jax.ShapeDtypeStruct((2 * all_req, columns), BF),
            jax.ShapeDtypeStruct((all_req, columns), F32),
        ]
    return pl.pallas_call(
        kernel,
        in_specs=in_specs,
        out_specs=[VMEM] * len(outs),
        out_shape=outs,
        scratch_shapes=scratch,
        compiler_params=small_params(ATTENTION_MIB),
        cost_estimate=EARLY,
        name="attention",
    )(*arrays)


def project(name, blocks, weights, extras, finish, outs, step=1024):
    rows = sum(x.shape[0] for x in blocks)
    depth, columns = weights.shape
    n = len(blocks)
    m = len(extras)

    def kernel(*refs):
        xs, w, more = refs[:n], refs[n], refs[n + 1 : n + 1 + m]
        results, total = refs[n + 1 + m : -1], refs[-1]
        for k in range(depth // step):
            part = slice(k * step, (k + 1) * step)
            x = jnp.concatenate([r[:, part] for r in xs], axis=0)
            term = jnp.dot(x, w[part], preferred_element_type=F32)
            if k == 0:
                total[...] = term
            else:
                total[...] += term
        finish(total, more, results)

    return pl.pallas_call(
        kernel,
        in_specs=[VMEM] * (n + 1 + m),
        out_specs=[VMEM] * len(outs),
        out_shape=outs,
        scratch_shapes=[pltpu.VMEM((rows, columns), F32)],
        compiler_params=small_params(),
        cost_estimate=EARLY,
        name=name,
    )(*blocks, weights, *extras)


def split_pairs(pairs, firsts, seconds, keep, send):
    position = coordinates(lax.axis_index("request"))[3]
    side = lax.axis_index("tensor")
    rows = keep.shape[0] // len(pairs)
    for i, pair in enumerate(pairs):
        mine = first_is_mine(pair, position, side)[1]
        u, v = firsts[i], seconds[i]
        keep[i * rows : (i + 1) * rows] = jnp.where(mine, u, v)
        send[i * rows : (i + 1) * rows] = jnp.where(mine, v, u).astype(BF)


def join_layer(name, layer, own, other, before, join, outs, finish, step=1024):
    depth, columns = join.shape[1:]
    steps = columns // (2 * step)

    def kernel(*refs):
        a_ref, b_ref, w0, w1 = refs[:4]
        x = (a_ref[...] + b_ref[...]).astype(BF)
        term = jnp.concatenate(
            [
                jnp.dot(x, w0[0], preferred_element_type=F32),
                jnp.dot(x, w1[0], preferred_element_type=F32),
            ],
            axis=1,
        )
        rest = refs[4:]
        if before is not None:
            term = term + rest[0][...]
            rest = rest[1:]
        finish(term, rest)

    rows = pl.BlockSpec((32, depth), lambda n: (0, 0))
    arrays = [own, other, join, join]
    specs = [
        rows,
        rows,
        pl.BlockSpec((1, depth, step), lambda n: (layer, 0, 2 * n)),
        pl.BlockSpec((1, depth, step), lambda n: (layer, 0, 2 * n + 1)),
    ]
    if before is not None:
        arrays.append(before)
        specs.append(pl.BlockSpec((32, 2 * step), lambda n: (0, n)))
    return pl.pallas_call(
        kernel,
        grid=(steps,),
        in_specs=specs,
        out_specs=[pl.BlockSpec((o.shape[0], 2 * step), lambda n: (0, n)) for o in outs],
        out_shape=outs,
        compiler_params=stream_params(),
        cost_estimate=EARLY,
        name=name,
    )(*arrays)


def project_and_join(name, blocks, weights, split, own, other, before, join, layer, step=1024):
    rows = sum(x.shape[0] for x in blocks)
    depth, columns = weights.shape
    count, joined = before.shape
    half = count // 2
    n = len(blocks)
    chunks = joined // step

    def kernel(*refs):
        xs, w, a_ref, b_ref, before_ref, j_hbm = refs[:n], *refs[n : n + 5]
        keep, send, keep_half, send_half, total, held, sem = refs[n + 5 :]
        copies = []
        for i in range(chunks):
            at = pl.ds(i * step, step)
            copies.append(
                pltpu.make_async_copy(j_hbm.at[layer, :, at], held.at[:, at], sem.at[i])
            )
            copies[-1].start()
        for k in range(depth // step):
            part = slice(k * step, (k + 1) * step)
            x = jnp.concatenate([r[:, part] for r in xs], axis=0)
            term = jnp.dot(x, w[part], preferred_element_type=F32)
            if k == 0:
                total[...] = term
            else:
                total[...] += term
        split(total, keep, send)
        x = (a_ref[...] + b_ref[...]).astype(BF)
        for i in range(chunks):
            part = slice(i * step, (i + 1) * step)
            copies[i].wait()
            term = jnp.dot(x, held[:, part], preferred_element_type=F32) + before_ref[:, part]
            keep_half[:, part] = term[:half]
            send_half[:, part] = term[half:].astype(BF)

    return pl.pallas_call(
        kernel,
        in_specs=[VMEM] * (n + 4) + [HBM],
        out_specs=[VMEM] * 4,
        out_shape=[
            jax.ShapeDtypeStruct((rows // 2, columns), F32),
            jax.ShapeDtypeStruct((rows // 2, columns), BF),
            jax.ShapeDtypeStruct((half, joined), F32),
            jax.ShapeDtypeStruct((half, joined), BF),
        ],
        scratch_shapes=[
            pltpu.VMEM((rows, columns), F32),
            pltpu.VMEM(join.shape[1:], BF),
            pltpu.SemaphoreType.DMA((chunks,)),
        ],
        compiler_params=small_params(22),
        cost_estimate=EARLY,
        name=name,
    )(*blocks, weights, own, other, before, join)


def finish_hidden(residual, kept, got):
    rows = 2 * TREE
    n = len(kept)
    pair_of = []
    for i, k in enumerate(kept):
        pair_of.append(k[1])
    arrays = [k[0] for k in kept] + list(got)

    def kernel(res, *refs):
        out = refs[-1]
        core, _, _, position = coordinates(lax.axis_index("request"))
        side = lax.axis_index("tensor")
        for i in range(n):
            keep, more = refs[i], refs[n + i]
            for j, pair in enumerate(pair_of[i]):
                first, mine = first_is_mine(pair, position, side)
                chip = jnp.where(mine, first, (first + 4) & 7)
                chip = jnp.where(chip < 4, chip * 2, (7 - chip) * 2 + 1)
                for c in range(2):
                    place = (chip * 2 + (core ^ c) - side * 8) * rows
                    place = pl.multiple_of(place, rows)
                    here = slice((2 * j + c) * rows, (2 * j + c + 1) * rows)
                    total = keep[here] + more[here].astype(F32)
                    out[pl.ds(place, rows)] = (res[pl.ds(place, rows)].astype(F32) + total).astype(BF)

    return pl.pallas_call(
        kernel,
        in_specs=[VMEM] * (1 + len(arrays)),
        out_specs=VMEM,
        out_shape=jax.ShapeDtypeStruct(residual.shape, BF),
        compiler_params=small_params(),
        cost_estimate=EARLY,
        name="finish_hidden",
    )(residual, *arrays)


def add_and_split(name, keep, got, pieces):
    rows, columns = keep.shape
    part = rows // pieces

    def kernel(k_ref, g_ref, stay_ref, *sends):
        total = k_ref[...] + g_ref[...].astype(F32)
        stay_ref[...] = total[:part]
        for i, s in enumerate(sends):
            s[...] = total[(i + 1) * part : (i + 2) * part].astype(BF)

    return pl.pallas_call(
        kernel,
        in_specs=[VMEM, VMEM],
        out_specs=[VMEM] * pieces,
        out_shape=[jax.ShapeDtypeStruct((part, columns), F32)]
        + [jax.ShapeDtypeStruct((part, columns), BF)] * (pieces - 1),
        compiler_params=small_params(),
        cost_estimate=EARLY,
        name=name,
    )(keep, got)


def tie(*values):
    return lax.optimization_barrier(values)


def ring_body(
    queries,
    cache_keys,
    cache_values,
    tree_keys,
    tree_values,
    cache_len,
    tree_parent,
    residual,
    low_feats,
    mid_feats,
    out_proj,
    last_node,
    draft_gain,
    draft_join,
):
    size = lax.axis_size("request")
    own_count = queries.shape[0]
    columns = residual.shape[2]
    width = draft_join.shape[2]
    all_req = last_node.shape[0]
    side_rows = residual.shape[0] * TREE
    block = own_count * TREE
    two = 2 * block

    forward = [(device_of(p, c), device_of(p + 1, c)) for p in range(CHIPS) for c in range(2)]
    backward = [(b, a) for a, b in forward]
    ahead = lambda v: lax.ppermute(v, "request", forward)
    back = lambda v: lax.ppermute(v, "request", backward)
    swap_core = lambda v: lax.ppermute(v, "request", [(r, r ^ 1) for r in range(size)])
    swap_x = lambda v: lax.ppermute(v, "request", [(r, r ^ 2) for r in range(size)])
    swap_z = lambda v, k: lax.ppermute(v, "request", [(r, r ^ (4 * k)) for r in range(size)])
    swap_side = lambda v: lax.ppermute(v, "tensor", [(0, 1), (1, 0)])
    f32 = lambda *shape: jax.ShapeDtypeStruct(shape, F32)
    bf16 = lambda *shape: jax.ShapeDtypeStruct(shape, BF)

    res = residual.reshape(-1, columns)
    h, picked, feats, res_rows = attention(
        queries,
        cache_keys,
        cache_values,
        tree_keys,
        tree_values,
        cache_len,
        tree_parent,
        last_node,
        picks=(low_feats.reshape(-1, columns), mid_feats.reshape(-1, columns), res),
    )
    feats_other = swap_side(feats)
    by_z = jnp.concatenate([picked, swap_z(picked, 1)], axis=0)
    h, by_z = tie(h, by_z)
    by_z = jnp.concatenate([by_z, swap_z(by_z, 2)], axis=0)
    f1, b1 = ahead(h), back(h)
    hs = swap_core(h)
    feats, feats_other, by_z = tie(feats, feats_other, by_z)
    by_x = jnp.concatenate([by_z, swap_x(by_z)], axis=0)
    store = lambda term, refs: refs[0].__setitem__(Ellipsis, term)
    (joined_low,) = join_layer(
        "join_low", 0, feats[:all_req], feats_other[:all_req], None, draft_join,
        [f32(all_req, width)], store,
    )

    f1, b1, hs, by_x, joined_low = tie(f1, b1, hs, by_x, joined_low)
    f2, b2 = ahead(f1), back(b1)
    picked_other = swap_core(by_x)
    f1s, b1s = swap_core(f1), swap_core(b1)

    def finish_a(total, more, results):
        results[0][...] = total[: 3 * two]
        results[1][...] = total[3 * two :] + more[0][...]

    part_a, part_picked = project(
        "project_a",
        [h, hs, f1, f1s, b1, b1s, by_x, picked_other],
        out_proj,
        [res_rows],
        finish_a,
        [f32(3 * two, columns), f32(all_req, columns)],
    )
    part_other = swap_side(part_picked)
    joined_low, part_a = tie(joined_low, part_a)
    (joined_feats,) = join_layer(
        "join_mid", 1, feats[all_req:], feats_other[all_req:], joined_low, draft_join,
        [f32(all_req, width)], store,
    )

    f2, b2, part_a, part_other, joined_feats = tie(f2, b2, part_a, part_other, joined_feats)
    f3, b3 = ahead(f2), back(b2)
    f2s, b2s = swap_core(f2), swap_core(b2)

    def split_2(total, keep, send):
        split_pairs([2], [total[:two]], [total[two:]], keep, send)

    keep_2, send_2, keep16, send16 = project_and_join(
        "project_2_join_hidden",
        [f2, f2s, b2, b2s],
        out_proj,
        split_2,
        part_picked,
        part_other,
        joined_feats,
        draft_join,
        2,
    )
    got16 = swap_core(send16)

    stay8, send8 = add_and_split("sum_core", keep16, got16, 2)
    f3, b3, stay8, send8, send_2 = tie(f3, b3, stay8, send8, send_2)
    got8 = swap_x(send8)
    got_2 = swap_side(send_2)
    f4, b4 = ahead(f3[:TREE]), back(b3[TREE:])
    f3s, b3s = swap_core(f3), swap_core(b3)

    def finish_3(total, more, results):
        before = more[0]
        split_pairs(
            [0, 1],
            [before[two : 2 * two], before[2 * two :]],
            [total[two:], total[:two]],
            *results,
        )

    keep_3, send_3 = project(
        "project_3", [f3, f3s, b3, b3s], out_proj, [part_a], finish_3,
        [f32(2 * two, columns), bf16(2 * two, columns)],
    )
    got_3 = swap_side(send_3)
    got8, keep_3 = tie(got8, keep_3)
    stay2, *sends = add_and_split("sum_x", stay8, got8, 4)

    f4, b4, got_2, *sends = tie(f4, b4, got_2, *sends)
    f4s, b4s = swap_core(f4), swap_core(b4)
    gots = [swap_z(v, k) for k, v in enumerate(sends, 1)]

    def finish_4(total, more, results):
        split_pairs([3], [more[0][:two]], [total[...]], *results)

    keep_4, send_4 = project(
        "project_4", [f4, b4, f4s, b4s], out_proj, [part_a], finish_4,
        [f32(two, columns), bf16(two, columns)],
    )
    got_4 = swap_side(send_4)
    keep_4, got_3, *gots = tie(keep_4, got_3, *gots)
    joined = stay2 + gots[0].astype(F32) + gots[1].astype(F32) + gots[2].astype(F32)
    squares = jnp.sum(joined * joined, axis=1, keepdims=True)
    other_squares = swap_side(squares)
    hidden = finish_hidden(
        res, [(keep_2, [2]), (keep_3, [0, 1]), (keep_4, [3])], [got_2, got_3, got_4]
    ).reshape(residual.shape)
    other_squares, hidden = tie(other_squares, hidden)
    row_scale = lax.rsqrt((squares + other_squares) / D + 1e-05)
    features = (joined * row_scale * draft_gain[None, :]).astype(BF)
    return (hidden, features)


def any_body(
    queries,
    cache_keys,
    cache_values,
    tree_keys,
    tree_values,
    cache_len,
    tree_parent,
    residual,
    low_feats,
    mid_feats,
    out_proj,
    last_node,
    draft_gain,
    draft_join,
):
    flat_rows, _ = attention(
        queries, cache_keys, cache_values, tree_keys, tree_values, cache_len, tree_parent, last_node
    )
    partial_value = jnp.dot(
        lax.all_gather(flat_rows, "request", axis=0, tiled=True),
        out_proj,
        preferred_element_type=F32,
    )
    summed = lax.psum_scatter(partial_value, "tensor", scatter_dimension=0, tiled=True)
    local_req = residual.shape[0]
    columns = residual.shape[2]
    hidden = (residual.reshape(-1, columns).astype(F32) + summed).astype(BF)
    hidden = hidden.reshape(residual.shape)
    first_req = lax.axis_index("tensor") * local_req
    chosen_all = last_node[:, None] == jnp.arange(TREE, dtype=jnp.int32)[None, :]
    own_chosen = lax.dynamic_slice_in_dim(chosen_all, first_req, local_req, 0)

    def choose(rows):
        return jnp.sum(jnp.where(own_chosen[:, :, None], rows.astype(F32), 0.0), axis=1).astype(BF)

    rows = jnp.stack((choose(low_feats), choose(mid_feats), choose(hidden)), axis=1)
    stacked = lax.all_gather(rows, "tensor", axis=0, tiled=True)
    joined_part = jnp.einsum("bsk,skn->bn", stacked, draft_join, preferred_element_type=F32)
    joined = lax.psum_scatter(joined_part, "request", scatter_dimension=0, tiled=True)
    squares = lax.psum(jnp.sum(joined * joined, axis=1), "tensor")
    row_scale = lax.rsqrt(squares / D + 1e-05)
    features = (joined * row_scale[:, None] * draft_gain[None, :]).astype(BF)
    return (hidden, features)


def solution(mesh):
    small = mesh.shape["tensor"] == 2 and mesh.shape["request"] == 2 * CHIPS
    return jax.shard_map(
        ring_body if small else any_body,
        mesh=mesh,
        in_specs=(
            P("request", None, "tensor"),
            P("request", None, "tensor"),
            P("request", None, "tensor"),
            P("request", None, "tensor"),
            P("request", None, "tensor"),
            P("request"),
            P("request", None),
            P("tensor", None, "request"),
            P("tensor", None, "request"),
            P("tensor", None, "request"),
            P("tensor", "request"),
            P(),
            P("tensor"),
            P(None, "request", "tensor"),
        ),
        out_specs=(P("tensor", None, "request"), P("request", "tensor")),
        check_vma=False,
    )
```

```python
import jax
import jax.numpy as jnp
from jax import lax
from jax.experimental import pallas as pl
from jax.experimental.pallas import tpu as pltpu
from jax.sharding import PartitionSpec as P

D = 16384
HEADS = 128
KV_HEADS = 8
HEAD = 128
TREE = 16
GROUP = HEADS // KV_HEADS
FACTOR = HEAD ** (-0.5)
MIB = 1024 * 1024
ATTENTION_MIB = 58
EARLY = pl.CostEstimate(flops=1, bytes_accessed=1, transcendentals=0)
BF = jnp.bfloat16
F32 = jnp.float32


def small_params(limit=12):
    return pltpu.CompilerParams(vmem_limit_bytes=int(limit * MIB))


def stream_params():
    return pltpu.CompilerParams(
        vmem_limit_bytes=16 * MIB, dimension_semantics=("arbitrary",)
    )


CHIPS = 8


def chip_of(position):
    return (position, 0) if position < 4 else (7 - position, 1)


def device_of(position, core):
    z, x = chip_of(position % CHIPS)
    return (z * 2 + x) * 2 + core


def coordinates(request):
    core, x, z = request & 1, (request >> 1) & 1, request >> 2
    return core, x, z, jnp.where(x == 0, z, 7 - z)


PAIRS = ((-1, 3), (1, -3), (-2, 2), (0, 4))


def first_is_mine(pair, position, side):
    first = (position + PAIRS[pair][0] + CHIPS) & 7
    return first, (((first + 2) >> 2) & 1) == side


HBM = pl.BlockSpec(memory_space=pltpu.HBM)
VMEM = pl.BlockSpec(memory_space=pltpu.VMEM)
SMEM = pl.BlockSpec(memory_space=pltpu.SMEM)


def attention(queries, ck, cv, tk, tv, lengths, parents, last, picks=None):
    count, _, width = queries.shape
    cache = ck.shape[1]
    groups = ck.shape[2] // HEAD
    lanes = GROUP * HEAD
    sources = (parents, queries, ck, tk, cv, tv) + (picks or ())
    all_req = last.shape[0]

    def kernel(len_ref, last_ref, *refs):
        n = len(sources)
        here, refs = refs[:n], refs[n:]
        if picks:
            row_ref, o_ref, pick_ref, feats_ref, res_out_ref = refs[:5]
            refs = refs[5:]
        else:
            o_ref, pick_ref = refs[:2]
            refs = refs[2:]
        held, sem = refs[:n], refs[n]
        copies = [pltpu.make_async_copy(a, v, sem.at[i]) for i, (a, v) in enumerate(zip(here, held))]
        for c in copies:
            c.start()
        parent, q_ref, ck_ref, tk_ref, cv_ref, tv_ref = held[:6]
        first = lax.axis_index("request") * count
        copies[0].wait()
        up = lax.broadcasted_iota(jnp.int32, (TREE, TREE), 0)
        node = lax.broadcasted_iota(jnp.int32, (TREE, TREE), 1)
        spread = lax.broadcasted_iota(jnp.int32, (TREE, GROUP * TREE), 1) % TREE
        spread = spread == lax.broadcasted_iota(jnp.int32, (TREE, GROUP * TREE), 0)
        spread = jnp.where(spread, 1.0, 0.0).astype(BF)
        dims = (((1,), (1,)), ((), ()))
        seen = []
        for b in range(count):
            reach = jnp.where((parent[b : b + 1] == up) | (up == node), 1.0, 0.0).astype(BF)
            for _ in range(4):
                paths = jnp.dot(reach, reach, preferred_element_type=F32)
                reach = jnp.minimum(paths, 1.0).astype(BF)
            seen.append(jnp.dot(reach, spread, preferred_element_type=F32) > 0.5)
        for c in copies[1:6]:
            c.wait()
        for b in range(count):
            live = lax.broadcasted_iota(jnp.int32, (cache, 1), 0) < len_ref[b]
            chosen = lax.broadcasted_iota(jnp.int32, (TREE, 1), 0) == last_ref[first + b]
            for g in range(groups):
                head = slice(g * HEAD, (g + 1) * HEAD)
                base = g * lanes
                q = jnp.concatenate(
                    [q_ref[b, :, base + h * HEAD : base + (h + 1) * HEAD] for h in range(GROUP)],
                    axis=0,
                )
                s_cache = lax.dot_general(ck_ref[b, :, head], q, dims, preferred_element_type=F32)
                s_tree = lax.dot_general(tk_ref[b, :, head], q, dims, preferred_element_type=F32)
                s_cache = jnp.where(live, s_cache * FACTOR, -1e30)
                s_tree = jnp.where(seen[b], s_tree * FACTOR, -1e30)
                top = jnp.maximum(
                    jnp.max(s_cache, axis=0, keepdims=True), jnp.max(s_tree, axis=0, keepdims=True)
                )
                e_cache = jnp.exp(s_cache - top)
                e_tree = jnp.exp(s_tree - top)
                total = jnp.sum(e_cache, axis=0, keepdims=True) + jnp.sum(
                    e_tree, axis=0, keepdims=True
                )
                inverse = 1.0 / total
                w_cache = (e_cache * inverse).astype(BF)
                w_tree = (e_tree * inverse).astype(BF)
                over = (((0,), (0,)), ((), ()))
                mixed = lax.dot_general(
                    w_cache, cv_ref[b, :, head], over, preferred_element_type=F32
                )
                mixed = mixed + lax.dot_general(
                    w_tree, tv_ref[b, :, head], over, preferred_element_type=F32
                )
                for h in range(GROUP):
                    block = mixed[h * TREE : (h + 1) * TREE]
                    where = slice(base + h * HEAD, base + (h + 1) * HEAD)
                    o_ref[b * TREE : (b + 1) * TREE, where] = block.astype(BF)
                    pick_ref[b : b + 1, where] = jnp.sum(
                        jnp.where(chosen, block, 0.0), axis=0, keepdims=True
                    ).astype(BF)

        if picks:
            side_rows = picks[0].shape[0]
            core, x, z, _ = coordinates(lax.axis_index("request"))
            order = lax.broadcasted_iota(jnp.int32, (all_req, all_req), 0)
            of_core, of_x = core ^ (order >> 4), x ^ ((order >> 3) & 1)
            of_z = z ^ ((order >> 1) & 3)
            req = ((of_z * 2 + of_x) * 2 + of_core) * count + (order & 1)
            named = req == lax.broadcasted_iota(jnp.int32, (all_req, all_req), 1)
            last_rel = jnp.sum(jnp.where(named, row_ref[...], 0), axis=1, keepdims=True)
            rows = req[:, :1] * TREE + last_rel - lax.axis_index("tensor") * side_rows
            hot = rows == lax.broadcasted_iota(jnp.int32, (all_req, side_rows), 1)
            hot = jnp.where(hot, 1.0, 0.0).astype(BF)
            for c in copies[6:9]:
                c.wait()
            for i in range(2):
                feats_ref[i * all_req : (i + 1) * all_req] = jnp.dot(
                    hot, held[6 + i][...], preferred_element_type=F32
                ).astype(BF)
            res_out_ref[...] = jnp.dot(hot, held[8][...], preferred_element_type=F32)

    arrays = [lengths, last, *sources]
    in_specs = [SMEM, SMEM] + [HBM] * len(sources)
    outs = [
        jax.ShapeDtypeStruct((count * TREE, width), BF),
        jax.ShapeDtypeStruct((count, width), BF),
    ]
    scratch = [pltpu.VMEM(a.shape, a.dtype) for a in sources]
    scratch.append(pltpu.SemaphoreType.DMA((len(sources),)))
    if picks:
        arrays.append(last[None, :])
        in_specs.append(VMEM)
        columns = picks[0].shape[1]
        outs += [
            jax.ShapeDtypeStruct((2 * all_req, columns), BF),
            jax.ShapeDtypeStruct((all_req, columns), F32),
        ]
    return pl.pallas_call(
        kernel,
        in_specs=in_specs,
        out_specs=[VMEM] * len(outs),
        out_shape=outs,
        scratch_shapes=scratch,
        compiler_params=small_params(ATTENTION_MIB),
        cost_estimate=EARLY,
        name="attention",
    )(*arrays)


def project(name, blocks, weights, extras, finish, outs, step=1024):
    rows = sum(x.shape[0] for x in blocks)
    depth, columns = weights.shape
    n = len(blocks)
    m = len(extras)

    def kernel(*refs):
        xs, w, more = refs[:n], refs[n], refs[n + 1 : n + 1 + m]
        results, total = refs[n + 1 + m : -1], refs[-1]
        for k in range(depth // step):
            part = slice(k * step, (k + 1) * step)
            x = jnp.concatenate([r[:, part] for r in xs], axis=0)
            term = jnp.dot(x, w[part], preferred_element_type=F32)
            if k == 0:
                total[...] = term
            else:
                total[...] += term
        finish(total, more, results)

    return pl.pallas_call(
        kernel,
        in_specs=[VMEM] * (n + 1 + m),
        out_specs=[VMEM] * len(outs),
        out_shape=outs,
        scratch_shapes=[pltpu.VMEM((rows, columns), F32)],
        compiler_params=small_params(),
        cost_estimate=EARLY,
        name=name,
    )(*blocks, weights, *extras)


def split_pairs(pairs, firsts, seconds, keep, send):
    position = coordinates(lax.axis_index("request"))[3]
    side = lax.axis_index("tensor")
    rows = keep.shape[0] // len(pairs)
    for i, pair in enumerate(pairs):
        mine = first_is_mine(pair, position, side)[1]
        u, v = firsts[i], seconds[i]
        keep[i * rows : (i + 1) * rows] = jnp.where(mine, u, v)
        send[i * rows : (i + 1) * rows] = jnp.where(mine, v, u).astype(BF)


def join_layer(name, layer, own, other, before, join, outs, finish, step=1024):
    depth, columns = join.shape[1:]
    steps = columns // (2 * step)

    def kernel(*refs):
        a_ref, b_ref, w0, w1 = refs[:4]
        x = (a_ref[...] + b_ref[...]).astype(BF)
        term = jnp.concatenate(
            [
                jnp.dot(x, w0[0], preferred_element_type=F32),
                jnp.dot(x, w1[0], preferred_element_type=F32),
            ],
            axis=1,
        )
        rest = refs[4:]
        if before is not None:
            term = term + rest[0][...]
            rest = rest[1:]
        finish(term, rest)

    rows = pl.BlockSpec((32, depth), lambda n: (0, 0))
    arrays = [own, other, join, join]
    specs = [
        rows,
        rows,
        pl.BlockSpec((1, depth, step), lambda n: (layer, 0, 2 * n)),
        pl.BlockSpec((1, depth, step), lambda n: (layer, 0, 2 * n + 1)),
    ]
    if before is not None:
        arrays.append(before)
        specs.append(pl.BlockSpec((32, 2 * step), lambda n: (0, n)))
    return pl.pallas_call(
        kernel,
        grid=(steps,),
        in_specs=specs,
        out_specs=[pl.BlockSpec((o.shape[0], 2 * step), lambda n: (0, n)) for o in outs],
        out_shape=outs,
        compiler_params=stream_params(),
        cost_estimate=EARLY,
        name=name,
    )(*arrays)


def project_and_join(name, blocks, weights, split, own, other, before, join, layer, step=1024):
    rows = sum(x.shape[0] for x in blocks)
    depth, columns = weights.shape
    count, joined = before.shape
    half = count // 2
    n = len(blocks)
    chunks = joined // step

    def kernel(*refs):
        xs, w, a_ref, b_ref, before_ref, j_hbm = refs[:n], *refs[n : n + 5]
        keep, send, keep_half, send_half, total, held, sem = refs[n + 5 :]
        copies = []
        for i in range(chunks):
            at = pl.ds(i * step, step)
            copies.append(
                pltpu.make_async_copy(j_hbm.at[layer, :, at], held.at[:, at], sem.at[i])
            )
            copies[-1].start()
        for k in range(depth // step):
            part = slice(k * step, (k + 1) * step)
            x = jnp.concatenate([r[:, part] for r in xs], axis=0)
            term = jnp.dot(x, w[part], preferred_element_type=F32)
            if k == 0:
                total[...] = term
            else:
                total[...] += term
        split(total, keep, send)
        x = (a_ref[...] + b_ref[...]).astype(BF)
        for i in range(chunks):
            part = slice(i * step, (i + 1) * step)
            copies[i].wait()
            term = jnp.dot(x, held[:, part], preferred_element_type=F32) + before_ref[:, part]
            keep_half[:, part] = term[:half]
            send_half[:, part] = term[half:].astype(BF)

    return pl.pallas_call(
        kernel,
        in_specs=[VMEM] * (n + 4) + [HBM],
        out_specs=[VMEM] * 4,
        out_shape=[
            jax.ShapeDtypeStruct((rows // 2, columns), F32),
            jax.ShapeDtypeStruct((rows // 2, columns), BF),
            jax.ShapeDtypeStruct((half, joined), F32),
            jax.ShapeDtypeStruct((half, joined), BF),
        ],
        scratch_shapes=[
            pltpu.VMEM((rows, columns), F32),
            pltpu.VMEM(join.shape[1:], BF),
            pltpu.SemaphoreType.DMA((chunks,)),
        ],
        compiler_params=small_params(22),
        cost_estimate=EARLY,
        name=name,
    )(*blocks, weights, own, other, before, join)


def finish_hidden(residual, kept, got):
    rows = 2 * TREE
    n = len(kept)
    pair_of = []
    for i, k in enumerate(kept):
        pair_of.append(k[1])
    arrays = [k[0] for k in kept] + list(got)

    def kernel(res, *refs):
        out = refs[-1]
        core, _, _, position = coordinates(lax.axis_index("request"))
        side = lax.axis_index("tensor")
        for i in range(n):
            keep, more = refs[i], refs[n + i]
            for j, pair in enumerate(pair_of[i]):
                first, mine = first_is_mine(pair, position, side)
                chip = jnp.where(mine, first, (first + 4) & 7)
                chip = jnp.where(chip < 4, chip * 2, (7 - chip) * 2 + 1)
                for c in range(2):
                    place = (chip * 2 + (core ^ c) - side * 8) * rows
                    place = pl.multiple_of(place, rows)
                    here = slice((2 * j + c) * rows, (2 * j + c + 1) * rows)
                    total = keep[here] + more[here].astype(F32)
                    out[pl.ds(place, rows)] = (res[pl.ds(place, rows)].astype(F32) + total).astype(BF)

    return pl.pallas_call(
        kernel,
        in_specs=[VMEM] * (1 + len(arrays)),
        out_specs=VMEM,
        out_shape=jax.ShapeDtypeStruct(residual.shape, BF),
        compiler_params=small_params(),
        cost_estimate=EARLY,
        name="finish_hidden",
    )(residual, *arrays)


def add_and_split(name, keep, got, pieces):
    rows, columns = keep.shape
    part = rows // pieces

    def kernel(k_ref, g_ref, stay_ref, *sends):
        total = k_ref[...] + g_ref[...].astype(F32)
        stay_ref[...] = total[:part]
        for i, s in enumerate(sends):
            s[...] = total[(i + 1) * part : (i + 2) * part].astype(BF)

    return pl.pallas_call(
        kernel,
        in_specs=[VMEM, VMEM],
        out_specs=[VMEM] * pieces,
        out_shape=[jax.ShapeDtypeStruct((part, columns), F32)]
        + [jax.ShapeDtypeStruct((part, columns), BF)] * (pieces - 1),
        compiler_params=small_params(),
        cost_estimate=EARLY,
        name=name,
    )(keep, got)


def tie(*values):
    return lax.optimization_barrier(values)


def ring_body(
    queries,
    cache_keys,
    cache_values,
    tree_keys,
    tree_values,
    cache_len,
    tree_parent,
    residual,
    low_feats,
    mid_feats,
    out_proj,
    last_node,
    draft_gain,
    draft_join,
):
    size = lax.axis_size("request")
    own_count = queries.shape[0]
    columns = residual.shape[2]
    width = draft_join.shape[2]
    all_req = last_node.shape[0]
    side_rows = residual.shape[0] * TREE
    block = own_count * TREE
    two = 2 * block

    forward = [(device_of(p, c), device_of(p + 1, c)) for p in range(CHIPS) for c in range(2)]
    backward = [(b, a) for a, b in forward]
    ahead = lambda v: lax.ppermute(v, "request", forward)
    back = lambda v: lax.ppermute(v, "request", backward)
    swap_core = lambda v: lax.ppermute(v, "request", [(r, r ^ 1) for r in range(size)])
    swap_x = lambda v: lax.ppermute(v, "request", [(r, r ^ 2) for r in range(size)])
    swap_z = lambda v, k: lax.ppermute(v, "request", [(r, r ^ (4 * k)) for r in range(size)])
    swap_side = lambda v: lax.ppermute(v, "tensor", [(0, 1), (1, 0)])
    f32 = lambda *shape: jax.ShapeDtypeStruct(shape, F32)
    bf16 = lambda *shape: jax.ShapeDtypeStruct(shape, BF)

    res = residual.reshape(-1, columns)
    h, picked, feats, res_rows = attention(
        queries,
        cache_keys,
        cache_values,
        tree_keys,
        tree_values,
        cache_len,
        tree_parent,
        last_node,
        picks=(low_feats.reshape(-1, columns), mid_feats.reshape(-1, columns), res),
    )
    feats_other = swap_side(feats)
    by_z = jnp.concatenate([picked, swap_z(picked, 1)], axis=0)
    h, by_z = tie(h, by_z)
    by_z = jnp.concatenate([by_z, swap_z(by_z, 2)], axis=0)
    f1, b1 = ahead(h), back(h)
    hs = swap_core(h)
    feats, feats_other, by_z = tie(feats, feats_other, by_z)
    by_x = jnp.concatenate([by_z, swap_x(by_z)], axis=0)
    store = lambda term, refs: refs[0].__setitem__(Ellipsis, term)
    (joined_low,) = join_layer(
        "join_low", 0, feats[:all_req], feats_other[:all_req], None, draft_join,
        [f32(all_req, width)], store,
    )

    f1, b1, hs, by_x, joined_low = tie(f1, b1, hs, by_x, joined_low)
    f2, b2 = ahead(f1), back(b1)
    picked_other = swap_core(by_x)
    f1s, b1s = swap_core(f1), swap_core(b1)

    def finish_a(total, more, results):
        results[0][...] = total[: 3 * two]
        results[1][...] = total[3 * two :] + more[0][...]

    part_a, part_picked = project(
        "project_a",
        [h, hs, f1, f1s, b1, b1s, by_x, picked_other],
        out_proj,
        [res_rows],
        finish_a,
        [f32(3 * two, columns), f32(all_req, columns)],
    )
    part_other = swap_side(part_picked)
    joined_low, part_a = tie(joined_low, part_a)
    (joined_feats,) = join_layer(
        "join_mid", 1, feats[all_req:], feats_other[all_req:], joined_low, draft_join,
        [f32(all_req, width)], store,
    )

    f2, b2, part_a, part_other, joined_feats = tie(f2, b2, part_a, part_other, joined_feats)
    f3, b3 = ahead(f2), back(b2)
    f2s, b2s = swap_core(f2), swap_core(b2)

    def split_2(total, keep, send):
        split_pairs([2], [total[:two]], [total[two:]], keep, send)

    keep_2, send_2, keep16, send16 = project_and_join(
        "project_2_join_hidden",
        [f2, f2s, b2, b2s],
        out_proj,
        split_2,
        part_picked,
        part_other,
        joined_feats,
        draft_join,
        2,
    )
    got16 = swap_core(send16)

    stay8, send8 = add_and_split("sum_core", keep16, got16, 2)
    f3, b3, stay8, send8, send_2 = tie(f3, b3, stay8, send8, send_2)
    got8 = swap_x(send8)
    got_2 = swap_side(send_2)
    f4, b4 = ahead(f3[:TREE]), back(b3[TREE:])
    f3s, b3s = swap_core(f3), swap_core(b3)

    def finish_3(total, more, results):
        before = more[0]
        split_pairs(
            [0, 1],
            [before[two : 2 * two], before[2 * two :]],
            [total[two:], total[:two]],
            *results,
        )

    keep_3, send_3 = project(
        "project_3", [f3, f3s, b3, b3s], out_proj, [part_a], finish_3,
        [f32(2 * two, columns), bf16(2 * two, columns)],
    )
    got_3 = swap_side(send_3)
    got8, keep_3 = tie(got8, keep_3)
    stay2, *sends = add_and_split("sum_x", stay8, got8, 4)

    f4, b4, got_2, *sends = tie(f4, b4, got_2, *sends)
    f4s, b4s = swap_core(f4), swap_core(b4)
    gots = [swap_z(v, k) for k, v in enumerate(sends, 1)]

    def finish_4(total, more, results):
        split_pairs([3], [more[0][:two]], [total[:two]], *results)

    keep_4, send_4 = project(
        "project_4", [f4, b4, f4s, b4s, f4, b4, f4s, b4s], out_proj, [part_a], finish_4,
        [f32(two, columns), bf16(two, columns)],
    )
    got_4 = swap_side(send_4)
    keep_4, got_3, *gots = tie(keep_4, got_3, *gots)
    joined = stay2 + gots[0].astype(F32) + gots[1].astype(F32) + gots[2].astype(F32)
    squares = jnp.sum(joined * joined, axis=1, keepdims=True)
    other_squares = swap_side(squares)
    hidden = finish_hidden(
        res, [(keep_2, [2]), (keep_3, [0, 1]), (keep_4, [3])], [got_2, got_3, got_4]
    ).reshape(residual.shape)
    other_squares, hidden = tie(other_squares, hidden)
    row_scale = lax.rsqrt((squares + other_squares) / D + 1e-05)
    features = (joined * row_scale * draft_gain[None, :]).astype(BF)
    return (hidden, features)


def any_body(
    queries,
    cache_keys,
    cache_values,
    tree_keys,
    tree_values,
    cache_len,
    tree_parent,
    residual,
    low_feats,
    mid_feats,
    out_proj,
    last_node,
    draft_gain,
    draft_join,
):
    flat_rows, _ = attention(
        queries, cache_keys, cache_values, tree_keys, tree_values, cache_len, tree_parent, last_node
    )
    partial_value = jnp.dot(
        lax.all_gather(flat_rows, "request", axis=0, tiled=True),
        out_proj,
        preferred_element_type=F32,
    )
    summed = lax.psum_scatter(partial_value, "tensor", scatter_dimension=0, tiled=True)
    local_req = residual.shape[0]
    columns = residual.shape[2]
    hidden = (residual.reshape(-1, columns).astype(F32) + summed).astype(BF)
    hidden = hidden.reshape(residual.shape)
    first_req = lax.axis_index("tensor") * local_req
    chosen_all = last_node[:, None] == jnp.arange(TREE, dtype=jnp.int32)[None, :]
    own_chosen = lax.dynamic_slice_in_dim(chosen_all, first_req, local_req, 0)

    def choose(rows):
        return jnp.sum(jnp.where(own_chosen[:, :, None], rows.astype(F32), 0.0), axis=1).astype(BF)

    rows = jnp.stack((choose(low_feats), choose(mid_feats), choose(hidden)), axis=1)
    stacked = lax.all_gather(rows, "tensor", axis=0, tiled=True)
    joined_part = jnp.einsum("bsk,skn->bn", stacked, draft_join, preferred_element_type=F32)
    joined = lax.psum_scatter(joined_part, "request", scatter_dimension=0, tiled=True)
    squares = lax.psum(jnp.sum(joined * joined, axis=1), "tensor")
    row_scale = lax.rsqrt(squares / D + 1e-05)
    features = (joined * row_scale[:, None] * draft_gain[None, :]).astype(BF)
    return (hidden, features)


def solution(mesh):
    small = mesh.shape["tensor"] == 2 and mesh.shape["request"] == 2 * CHIPS
    return jax.shard_map(
        ring_body if small else any_body,
        mesh=mesh,
        in_specs=(
            P("request", None, "tensor"),
            P("request", None, "tensor"),
            P("request", None, "tensor"),
            P("request", None, "tensor"),
            P("request", None, "tensor"),
            P("request"),
            P("request", None),
            P("tensor", None, "request"),
            P("tensor", None, "request"),
            P("tensor", None, "request"),
            P("tensor", "request"),
            P(),
            P("tensor"),
            P(None, "request", "tensor"),
        ),
        out_specs=(P("tensor", None, "request"), P("request", "tensor")),
        check_vma=False,
    )
```

```python
import jax
import jax.numpy as jnp
from jax import lax
from jax.experimental import pallas as pl
from jax.experimental.pallas import tpu as pltpu
from jax.sharding import PartitionSpec as P

D = 16384
HEADS = 128
KV_HEADS = 8
HEAD = 128
TREE = 16
GROUP = HEADS // KV_HEADS
FACTOR = HEAD ** (-0.5)
MIB = 1024 * 1024
ATTENTION_MIB = 58
EARLY = pl.CostEstimate(flops=1, bytes_accessed=1, transcendentals=0)
BF = jnp.bfloat16
F32 = jnp.float32


def small_params(limit=12):
    return pltpu.CompilerParams(vmem_limit_bytes=int(limit * MIB))


def stream_params():
    return pltpu.CompilerParams(
        vmem_limit_bytes=16 * MIB, dimension_semantics=("arbitrary",)
    )


CHIPS = 8


def chip_of(position):
    return (position, 0) if position < 4 else (7 - position, 1)


def device_of(position, core):
    z, x = chip_of(position % CHIPS)
    return (z * 2 + x) * 2 + core


def coordinates(request):
    core, x, z = request & 1, (request >> 1) & 1, request >> 2
    return core, x, z, jnp.where(x == 0, z, 7 - z)


PAIRS = ((-1, 3), (1, -3), (-2, 2), (0, 4))


def first_is_mine(pair, position, side):
    first = (position + PAIRS[pair][0] + CHIPS) & 7
    return first, (((first + 2) >> 2) & 1) == side


HBM = pl.BlockSpec(memory_space=pltpu.HBM)
VMEM = pl.BlockSpec(memory_space=pltpu.VMEM)
SMEM = pl.BlockSpec(memory_space=pltpu.SMEM)


def attention(queries, ck, cv, tk, tv, lengths, parents, last, picks=None):
    count, _, width = queries.shape
    cache = ck.shape[1]
    groups = ck.shape[2] // HEAD
    lanes = GROUP * HEAD
    sources = (parents, queries, ck, tk, cv, tv) + (picks or ())
    all_req = last.shape[0]

    def kernel(len_ref, last_ref, *refs):
        n = len(sources)
        here, refs = refs[:n], refs[n:]
        if picks:
            row_ref, o_ref, pick_ref, feats_ref, res_out_ref = refs[:5]
            refs = refs[5:]
        else:
            o_ref, pick_ref = refs[:2]
            refs = refs[2:]
        held, sem = refs[:n], refs[n]
        copies = [pltpu.make_async_copy(a, v, sem.at[i]) for i, (a, v) in enumerate(zip(here, held))]
        for c in copies:
            c.start()
        parent, q_ref, ck_ref, tk_ref, cv_ref, tv_ref = held[:6]
        first = lax.axis_index("request") * count
        copies[0].wait()
        up = lax.broadcasted_iota(jnp.int32, (TREE, TREE), 0)
        node = lax.broadcasted_iota(jnp.int32, (TREE, TREE), 1)
        spread = lax.broadcasted_iota(jnp.int32, (TREE, GROUP * TREE), 1) % TREE
        spread = spread == lax.broadcasted_iota(jnp.int32, (TREE, GROUP * TREE), 0)
        spread = jnp.where(spread, 1.0, 0.0).astype(BF)
        dims = (((1,), (1,)), ((), ()))
        seen = []
        for b in range(count):
            reach = jnp.where((parent[b : b + 1] == up) | (up == node), 1.0, 0.0).astype(BF)
            for _ in range(4):
                paths = jnp.dot(reach, reach, preferred_element_type=F32)
                reach = jnp.minimum(paths, 1.0).astype(BF)
            seen.append(jnp.dot(reach, spread, preferred_element_type=F32) > 0.5)
        for c in copies[1:6]:
            c.wait()
        for b in range(count):
            live = lax.broadcasted_iota(jnp.int32, (cache, 1), 0) < len_ref[b]
            chosen = lax.broadcasted_iota(jnp.int32, (TREE, 1), 0) == last_ref[first + b]
            for g in range(groups):
                head = slice(g * HEAD, (g + 1) * HEAD)
                base = g * lanes
                q = jnp.concatenate(
                    [q_ref[b, :, base + h * HEAD : base + (h + 1) * HEAD] for h in range(GROUP)],
                    axis=0,
                )
                s_cache = lax.dot_general(ck_ref[b, :, head], q, dims, preferred_element_type=F32)
                s_tree = lax.dot_general(tk_ref[b, :, head], q, dims, preferred_element_type=F32)
                s_cache = jnp.where(live, s_cache * FACTOR, -1e30)
                s_tree = jnp.where(seen[b], s_tree * FACTOR, -1e30)
                top = jnp.maximum(
                    jnp.max(s_cache, axis=0, keepdims=True), jnp.max(s_tree, axis=0, keepdims=True)
                )
                e_cache = jnp.exp(s_cache - top)
                e_tree = jnp.exp(s_tree - top)
                total = jnp.sum(e_cache, axis=0, keepdims=True) + jnp.sum(
                    e_tree, axis=0, keepdims=True
                )
                inverse = 1.0 / total
                w_cache = (e_cache * inverse).astype(BF)
                w_tree = (e_tree * inverse).astype(BF)
                over = (((0,), (0,)), ((), ()))
                mixed = lax.dot_general(
                    w_cache, cv_ref[b, :, head], over, preferred_element_type=F32
                )
                mixed = mixed + lax.dot_general(
                    w_tree, tv_ref[b, :, head], over, preferred_element_type=F32
                )
                for h in range(GROUP):
                    block = mixed[h * TREE : (h + 1) * TREE]
                    where = slice(base + h * HEAD, base + (h + 1) * HEAD)
                    o_ref[b * TREE : (b + 1) * TREE, where] = block.astype(BF)
                    pick_ref[b : b + 1, where] = jnp.sum(
                        jnp.where(chosen, block, 0.0), axis=0, keepdims=True
                    ).astype(BF)

        if picks:
            side_rows = picks[0].shape[0]
            core, x, z, _ = coordinates(lax.axis_index("request"))
            order = lax.broadcasted_iota(jnp.int32, (all_req, all_req), 0)
            of_core, of_x = core ^ (order >> 4), x ^ ((order >> 3) & 1)
            of_z = z ^ ((order >> 1) & 3)
            req = ((of_z * 2 + of_x) * 2 + of_core) * count + (order & 1)
            named = req == lax.broadcasted_iota(jnp.int32, (all_req, all_req), 1)
            last_rel = jnp.sum(jnp.where(named, row_ref[...], 0), axis=1, keepdims=True)
            rows = req[:, :1] * TREE + last_rel - lax.axis_index("tensor") * side_rows
            hot = rows == lax.broadcasted_iota(jnp.int32, (all_req, side_rows), 1)
            hot = jnp.where(hot, 1.0, 0.0).astype(BF)
            for c in copies[6:9]:
                c.wait()
            for i in range(2):
                feats_ref[i * all_req : (i + 1) * all_req] = jnp.dot(
                    hot, held[6 + i][...], preferred_element_type=F32
                ).astype(BF)
            res_out_ref[...] = jnp.dot(hot, held[8][...], preferred_element_type=F32)

    arrays = [lengths, last, *sources]
    in_specs = [SMEM, SMEM] + [HBM] * len(sources)
    outs = [
        jax.ShapeDtypeStruct((count * TREE, width), BF),
        jax.ShapeDtypeStruct((count, width), BF),
    ]
    scratch = [pltpu.VMEM(a.shape, a.dtype) for a in sources]
    scratch.append(pltpu.SemaphoreType.DMA((len(sources),)))
    if picks:
        arrays.append(last[None, :])
        in_specs.append(VMEM)
        columns = picks[0].shape[1]
        outs += [
            jax.ShapeDtypeStruct((2 * all_req, columns), BF),
            jax.ShapeDtypeStruct((all_req, columns), F32),
        ]
    return pl.pallas_call(
        kernel,
        in_specs=in_specs,
        out_specs=[VMEM] * len(outs),
        out_shape=outs,
        scratch_shapes=scratch,
        compiler_params=small_params(ATTENTION_MIB),
        cost_estimate=EARLY,
        name="attention",
    )(*arrays)


def project(name, blocks, weights, extras, finish, outs, step=1024):
    rows = sum(x.shape[0] for x in blocks)
    depth, columns = weights.shape
    n = len(blocks)
    m = len(extras)

    def kernel(*refs):
        xs, w, more = refs[:n], refs[n], refs[n + 1 : n + 1 + m]
        results, total = refs[n + 1 + m : -1], refs[-1]
        for k in range(depth // step):
            part = slice(k * step, (k + 1) * step)
            x = jnp.concatenate([r[:, part] for r in xs], axis=0)
            term = jnp.dot(x, w[part], preferred_element_type=F32)
            if k == 0:
                total[...] = term
            else:
                total[...] += term
        finish(total, more, results)

    return pl.pallas_call(
        kernel,
        in_specs=[VMEM] * (n + 1 + m),
        out_specs=[VMEM] * len(outs),
        out_shape=outs,
        scratch_shapes=[pltpu.VMEM((rows, columns), F32)],
        compiler_params=small_params(),
        cost_estimate=EARLY,
        name=name,
    )(*blocks, weights, *extras)


def split_pairs(pairs, firsts, seconds, keep, send):
    position = coordinates(lax.axis_index("request"))[3]
    side = lax.axis_index("tensor")
    rows = keep.shape[0] // len(pairs)
    for i, pair in enumerate(pairs):
        mine = first_is_mine(pair, position, side)[1]
        u, v = firsts[i], seconds[i]
        keep[i * rows : (i + 1) * rows] = jnp.where(mine, u, v)
        send[i * rows : (i + 1) * rows] = jnp.where(mine, v, u).astype(BF)


def join_layer(name, layer, own, other, before, join, outs, finish, step=1024):
    depth, columns = join.shape[1:]
    steps = columns // (2 * step)

    def kernel(*refs):
        a_ref, b_ref, w0, w1 = refs[:4]
        x = (a_ref[...] + b_ref[...]).astype(BF)
        term = jnp.concatenate(
            [
                jnp.dot(x, w0[0], preferred_element_type=F32),
                jnp.dot(x, w1[0], preferred_element_type=F32),
            ],
            axis=1,
        )
        rest = refs[4:]
        if before is not None:
            term = term + rest[0][...]
            rest = rest[1:]
        finish(term, rest)

    rows = pl.BlockSpec((32, depth), lambda n: (0, 0))
    arrays = [own, other, join, join]
    specs = [
        rows,
        rows,
        pl.BlockSpec((1, depth, step), lambda n: (layer, 0, 2 * n)),
        pl.BlockSpec((1, depth, step), lambda n: (layer, 0, 2 * n + 1)),
    ]
    if before is not None:
        arrays.append(before)
        specs.append(pl.BlockSpec((32, 2 * step), lambda n: (0, n)))
    return pl.pallas_call(
        kernel,
        grid=(steps,),
        in_specs=specs,
        out_specs=[pl.BlockSpec((o.shape[0], 2 * step), lambda n: (0, n)) for o in outs],
        out_shape=outs,
        compiler_params=stream_params(),
        cost_estimate=EARLY,
        name=name,
    )(*arrays)


def project_and_join(name, blocks, weights, split, own, other, before, join, layer, step=1024):
    rows = sum(x.shape[0] for x in blocks)
    depth, columns = weights.shape
    count, joined = before.shape
    half = count // 2
    n = len(blocks)
    chunks = joined // step

    def kernel(*refs):
        xs, w, a_ref, b_ref, before_ref, j_hbm = refs[:n], *refs[n : n + 5]
        keep, send, keep_half, send_half, total, held, sem = refs[n + 5 :]
        copies = []
        for i in range(chunks):
            at = pl.ds(i * step, step)
            copies.append(
                pltpu.make_async_copy(j_hbm.at[layer, :, at], held.at[:, at], sem.at[i])
            )
            copies[-1].start()
        for k in range(depth // step):
            part = slice(k * step, (k + 1) * step)
            x = jnp.concatenate([r[:, part] for r in xs], axis=0)
            term = jnp.dot(x, w[part], preferred_element_type=F32)
            if k == 0:
                total[...] = term
            else:
                total[...] += term
        split(total, keep, send)
        x = (a_ref[...] + b_ref[...]).astype(BF)
        for i in range(chunks):
            part = slice(i * step, (i + 1) * step)
            copies[i].wait()
            term = jnp.dot(x, held[:, part], preferred_element_type=F32) + before_ref[:, part]
            keep_half[:, part] = term[:half]
            send_half[:, part] = term[half:].astype(BF)

    return pl.pallas_call(
        kernel,
        in_specs=[VMEM] * (n + 4) + [HBM],
        out_specs=[VMEM] * 4,
        out_shape=[
            jax.ShapeDtypeStruct((rows // 2, columns), F32),
            jax.ShapeDtypeStruct((rows // 2, columns), BF),
            jax.ShapeDtypeStruct((half, joined), F32),
            jax.ShapeDtypeStruct((half, joined), BF),
        ],
        scratch_shapes=[
            pltpu.VMEM((rows, columns), F32),
            pltpu.VMEM(join.shape[1:], BF),
            pltpu.SemaphoreType.DMA((chunks,)),
        ],
        compiler_params=small_params(22),
        cost_estimate=EARLY,
        name=name,
    )(*blocks, weights, own, other, before, join)


def finish_hidden(residual, kept, got):
    rows = 2 * TREE
    n = len(kept)
    arrays = [k[0] for k in kept] + [g[0] for g in got]

    def kernel(res, *refs):
        out = refs[-1]
        core, _, _, position = coordinates(lax.axis_index("request"))
        side = lax.axis_index("tensor")
        for i in range(n):
            keep, more = refs[i], refs[n + i]
            for j, pair in enumerate(kept[i][1]):
                first, mine = first_is_mine(pair, position, side)
                chip = jnp.where(mine, first, (first + 4) & 7)
                chip = jnp.where(chip < 4, chip * 2, (7 - chip) * 2 + 1)
                for c in range(2):
                    place = (chip * 2 + (core ^ c) - side * 8) * rows
                    place = pl.ds(pl.multiple_of(place, rows), rows)
                    at = (2 * j + c) * rows
                    total = keep[at : at + rows]
                    at = at + got[i][1]
                    total = total + more[at : at + rows].astype(F32)
                    out[place] = (res[place].astype(F32) + total).astype(BF)

    return pl.pallas_call(
        kernel,
        in_specs=[VMEM] * (1 + len(arrays)),
        out_specs=VMEM,
        out_shape=jax.ShapeDtypeStruct(residual.shape, BF),
        compiler_params=small_params(),
        cost_estimate=EARLY,
        name="finish_hidden",
    )(residual, *arrays)


def add_and_split(name, keep, got, pieces):
    rows, columns = keep.shape
    part = rows // pieces

    def kernel(k_ref, g_ref, stay_ref, *sends):
        total = k_ref[...] + g_ref[...].astype(F32)
        stay_ref[...] = total[:part]
        for i, s in enumerate(sends):
            s[...] = total[(i + 1) * part : (i + 2) * part].astype(BF)

    return pl.pallas_call(
        kernel,
        in_specs=[VMEM, VMEM],
        out_specs=[VMEM] * pieces,
        out_shape=[jax.ShapeDtypeStruct((part, columns), F32)]
        + [jax.ShapeDtypeStruct((part, columns), BF)] * (pieces - 1),
        compiler_params=small_params(),
        cost_estimate=EARLY,
        name=name,
    )(keep, got)


def tie(*values):
    return lax.optimization_barrier(values)


def ring_body(
    queries,
    cache_keys,
    cache_values,
    tree_keys,
    tree_values,
    cache_len,
    tree_parent,
    residual,
    low_feats,
    mid_feats,
    out_proj,
    last_node,
    draft_gain,
    draft_join,
):
    size = lax.axis_size("request")
    own_count = queries.shape[0]
    columns = residual.shape[2]
    width = draft_join.shape[2]
    all_req = last_node.shape[0]
    side_rows = residual.shape[0] * TREE
    block = own_count * TREE
    two = 2 * block

    forward = [(device_of(p, c), device_of(p + 1, c)) for p in range(CHIPS) for c in range(2)]
    backward = [(b, a) for a, b in forward]
    ahead = lambda v: lax.ppermute(v, "request", forward)
    back = lambda v: lax.ppermute(v, "request", backward)
    swap_core = lambda v: lax.ppermute(v, "request", [(r, r ^ 1) for r in range(size)])
    swap_x = lambda v: lax.ppermute(v, "request", [(r, r ^ 2) for r in range(size)])
    swap_z = lambda v, k: lax.ppermute(v, "request", [(r, r ^ (4 * k)) for r in range(size)])
    swap_side = lambda v: lax.ppermute(v, "tensor", [(0, 1), (1, 0)])
    f32 = lambda *shape: jax.ShapeDtypeStruct(shape, F32)
    bf16 = lambda *shape: jax.ShapeDtypeStruct(shape, BF)

    res = residual.reshape(-1, columns)
    h, picked, feats, res_rows = attention(
        queries,
        cache_keys,
        cache_values,
        tree_keys,
        tree_values,
        cache_len,
        tree_parent,
        last_node,
        picks=(low_feats.reshape(-1, columns), mid_feats.reshape(-1, columns), res),
    )
    feats_other = swap_side(feats)
    by_z = jnp.concatenate([picked, swap_z(picked, 1)], axis=0)
    h, by_z = tie(h, by_z)
    by_z = jnp.concatenate([by_z, swap_z(by_z, 2)], axis=0)
    f1, b1 = ahead(h), back(h)
    hs = swap_core(h)
    feats, feats_other, by_z = tie(feats, feats_other, by_z)
    by_x = jnp.concatenate([by_z, swap_x(by_z)], axis=0)
    store = lambda term, refs: refs[0].__setitem__(Ellipsis, term)
    (joined_low,) = join_layer(
        "join_low", 0, feats[:all_req], feats_other[:all_req], None, draft_join,
        [f32(all_req, width)], store,
    )

    f1, b1, hs, by_x, joined_low = tie(f1, b1, hs, by_x, joined_low)
    f2, b2 = ahead(f1), back(b1)
    picked_other = swap_core(by_x)
    f1s, b1s = swap_core(f1), swap_core(b1)

    def finish_a(total, more, results):
        results[0][...] = total[: 3 * two]
        results[1][...] = total[3 * two :] + more[0][...]

    part_a, part_picked = project(
        "project_a",
        [h, hs, f1, f1s, b1, b1s, by_x, picked_other],
        out_proj,
        [res_rows],
        finish_a,
        [f32(3 * two, columns), f32(all_req, columns)],
    )
    part_other = swap_side(part_picked)
    joined_low, part_a = tie(joined_low, part_a)
    (joined_feats,) = join_layer(
        "join_mid", 1, feats[all_req:], feats_other[all_req:], joined_low, draft_join,
        [f32(all_req, width)], store,
    )

    f2, b2, part_a, part_other, joined_feats = tie(f2, b2, part_a, part_other, joined_feats)
    f3, b3 = ahead(f2), back(b2)
    f2s, b2s = swap_core(f2), swap_core(b2)

    def split_2(total, keep, send):
        split_pairs([2], [total[:two]], [total[two:]], keep, send)

    keep_2, send_2, keep16, send16 = project_and_join(
        "project_2_join_hidden",
        [f2, f2s, b2, b2s],
        out_proj,
        split_2,
        part_picked,
        part_other,
        joined_feats,
        draft_join,
        2,
    )
    got16 = swap_core(send16)

    stay8, send8 = add_and_split("sum_core", keep16, got16, 2)
    f3, b3, stay8, send8, send_2 = tie(f3, b3, stay8, send8, send_2)
    got8 = swap_x(send8)
    f4, b4 = ahead(f3[:TREE]), back(b3[TREE:])
    f3s, b3s = swap_core(f3), swap_core(b3)

    def finish_3(total, more, results):
        before, earlier = more
        keep, send = results
        split_pairs(
            [0, 1],
            [before[two : 2 * two], before[2 * two :]],
            [total[two:], total[:two]],
            keep,
            send.at[: 2 * two],
        )
        send[2 * two :] = earlier[...]

    keep_3, send_3 = project(
        "project_3", [f3, f3s, b3, b3s], out_proj, [part_a, send_2], finish_3,
        [f32(2 * two, columns), bf16(3 * two, columns)],
    )
    got_3 = swap_side(send_3)
    got8, keep_3 = tie(got8, keep_3)
    stay2, *sends = add_and_split("sum_x", stay8, got8, 4)

    f4, b4, *sends = tie(f4, b4, *sends)
    f4s, b4s = swap_core(f4), swap_core(b4)
    gots = [swap_z(v, k) for k, v in enumerate(sends, 1)]

    def finish_4(total, more, results):
        split_pairs([3], [more[0][:two]], [total[:two]], *results)

    keep_4, send_4 = project(
        "project_4", [f4, b4, f4s, b4s, f4, b4, f4s, b4s], out_proj, [part_a], finish_4,
        [f32(two, columns), bf16(two, columns)],
    )
    got_4 = swap_side(send_4)
    keep_4, got_3, *gots = tie(keep_4, got_3, *gots)
    joined = stay2 + gots[0].astype(F32) + gots[1].astype(F32) + gots[2].astype(F32)
    squares = jnp.sum(joined * joined, axis=1, keepdims=True)
    other_squares = swap_side(squares)
    hidden = finish_hidden(
        res,
        [(keep_2, [2]), (keep_3, [0, 1]), (keep_4, [3])],
        [(got_3, 2 * two), (got_3, 0), (got_4, 0)],
    ).reshape(residual.shape)
    other_squares, hidden = tie(other_squares, hidden)
    row_scale = lax.rsqrt((squares + other_squares) / D + 1e-05)
    features = (joined * row_scale * draft_gain[None, :]).astype(BF)
    return (hidden, features)


def any_body(
    queries,
    cache_keys,
    cache_values,
    tree_keys,
    tree_values,
    cache_len,
    tree_parent,
    residual,
    low_feats,
    mid_feats,
    out_proj,
    last_node,
    draft_gain,
    draft_join,
):
    flat_rows, _ = attention(
        queries, cache_keys, cache_values, tree_keys, tree_values, cache_len, tree_parent, last_node
    )
    partial_value = jnp.dot(
        lax.all_gather(flat_rows, "request", axis=0, tiled=True),
        out_proj,
        preferred_element_type=F32,
    )
    summed = lax.psum_scatter(partial_value, "tensor", scatter_dimension=0, tiled=True)
    local_req = residual.shape[0]
    columns = residual.shape[2]
    hidden = (residual.reshape(-1, columns).astype(F32) + summed).astype(BF)
    hidden = hidden.reshape(residual.shape)
    first_req = lax.axis_index("tensor") * local_req
    chosen_all = last_node[:, None] == jnp.arange(TREE, dtype=jnp.int32)[None, :]
    own_chosen = lax.dynamic_slice_in_dim(chosen_all, first_req, local_req, 0)

    def choose(rows):
        return jnp.sum(jnp.where(own_chosen[:, :, None], rows.astype(F32), 0.0), axis=1).astype(BF)

    rows = jnp.stack((choose(low_feats), choose(mid_feats), choose(hidden)), axis=1)
    stacked = lax.all_gather(rows, "tensor", axis=0, tiled=True)
    joined_part = jnp.einsum("bsk,skn->bn", stacked, draft_join, preferred_element_type=F32)
    joined = lax.psum_scatter(joined_part, "request", scatter_dimension=0, tiled=True)
    squares = lax.psum(jnp.sum(joined * joined, axis=1), "tensor")
    row_scale = lax.rsqrt(squares / D + 1e-05)
    features = (joined * row_scale[:, None] * draft_gain[None, :]).astype(BF)
    return (hidden, features)


def solution(mesh):
    small = mesh.shape["tensor"] == 2 and mesh.shape["request"] == 2 * CHIPS
    return jax.shard_map(
        ring_body if small else any_body,
        mesh=mesh,
        in_specs=(
            P("request", None, "tensor"),
            P("request", None, "tensor"),
            P("request", None, "tensor"),
            P("request", None, "tensor"),
            P("request", None, "tensor"),
            P("request"),
            P("request", None),
            P("tensor", None, "request"),
            P("tensor", None, "request"),
            P("tensor", None, "request"),
            P("tensor", "request"),
            P(),
            P("tensor"),
            P(None, "request", "tensor"),
        ),
        out_specs=(P("tensor", None, "request"), P("request", "tensor")),
        check_vma=False,
    )
```
